1024 devices in a mesh: tm: 64 (over x, y_lo, core), row: 2 (over y_hi), col: 8 (over z).
Axes of the slice: x: 8, y: 8 (y_hi: 2, y_lo: 4; y = y_hi * 4 + y_lo), z: 8, core: 2. Of those that a mesh axis runs over, the one named last changes fastest.
Arguments:
- query: bfloat16 [64, 16, 128, 1024], P('tm', 'row', 'col'), may hold values from -6 to 6
- key: bfloat16 [64, 16, 128, 1024], P('tm', 'row', 'col'), may hold values from -6 to 6
- value: bfloat16 [64, 16, 128, 1024], P('tm', 'row', 'col'), may hold values from -6 to 6
- out_grad: bfloat16 [64, 16, 128, 1024], P('tm', 'row', 'col'), may hold values from -6 to 6
- tile_window: int32 [64, 2, 9], replicated, may hold values 0 or 1
- period_link: int32 [64], replicated, may hold values from 0 to 1, as said below
Outputs:
- attn_out: bfloat16 [64, 16, 128, 1024], P('tm', 'row', 'col')
- query_grad: bfloat16 [64, 16, 128, 1024], P('tm', 'row', 'col')
- key_grad: bfloat16 [64, 16, 128, 1024], P('tm', 'row', 'col')
- value_grad: bfloat16 [64, 16, 128, 1024], P('tm', 'row', 'col')
The draws below stay inside these ranges and needn't reach their ends.
Inputs may be any that keep to these rules, and one draw needn't show every extreme that they name: `period_link`: among periods 1 to 63 at least one has link 0 and at least one has link 1.
All inputs are finite; a program needn't handle non-finite values.
Results may differ from the reference program's by a relative error of at most 0.035.
Values may be sent and summed in bfloat16 or wider, within the bound.
A program may use at most 64 MiB of HBM per device.

```python
import math
import jax
import jax.numpy as jnp
from jax import lax

HEADS = 8
HD = 128
S = 4
FR = 1
PERIODS = 64
FRAMES = 64
HEIGHT = 16
WIDTH = 128
CHANNELS = 1024


def drawn_draw(key, salt):
    shape = (FRAMES, HEIGHT, WIDTH, HEADS * HD)
    own_key = jax.random.fold_in(key, salt)
    result = jax.random.truncated_normal(jax.random.fold_in(own_key, 5), -6.0, 6.0, shape)
    return result.astype(jnp.float32).astype(jnp.bfloat16)


def draw_query(key, part):
    return drawn_draw(key, 11)


def draw_key(key, part):
    return drawn_draw(key, 23)


def draw_period_link(key, part):
    key = jax.random.fold_in(key, 37)
    bits = jax.random.randint(jax.random.fold_in(key, 1), (PERIODS,), 0, 2).astype(jnp.int32)
    order = jax.random.permutation(jax.random.fold_in(key, 2), PERIODS - 1).astype(jnp.int32) + 1
    places = jnp.arange(PERIODS, dtype=jnp.int32)
    bits = jnp.where(places == order[0], 0, bits)
    bits = jnp.where(places == order[1], 1, bits)
    return bits.astype(jnp.int32)


def place_ends(entries, stream_key, smallest, high):
    place = [jax.random.randint(jax.random.fold_in(stream_key, axis), (), 0, length) for axis, length in enumerate(entries.shape)]
    longest = entries.shape.index(max(entries.shape))
    beside = place[:longest] + [(place[longest] + 1) % entries.shape[longest]] + place[longest + 1:]
    return entries.at[tuple(place)].set(smallest).at[tuple(beside)].set(high)


def levels(stream_key, extent, cuts, smallest, top_value):
    def one(axis_at, blocks):
        steps = jax.random.uniform(jax.random.fold_in(jax.random.fold_in(stream_key, 6), axis_at), (blocks,), jnp.float32, smallest / len(cuts), top_value / len(cuts))
        return jnp.repeat(jnp.exp(steps), extent[axis_at] // blocks).reshape((-1,) + (1,) * (len(extent) - axis_at - 1))

    gain = one(*cuts[0])
    for cut in cuts[1:]:
        gain = gain * one(*cut)
    return gain


def bell_draw(rng, shape, scale, reach, cuts=(), held_as=jnp.bfloat16):
    loudness = levels(rng, shape, cuts, -0.22, 0.18) if cuts else 1.0
    values = jax.random.normal(rng, shape, jnp.float32) * scale * loudness
    return jnp.minimum(jnp.maximum(values, -reach), reach).astype(held_as)


def setup_inputs(seed: int = 0) -> dict:
    keys = jax.random.split(jax.random.key(seed), 7)
    query = draw_query(jax.random.fold_in(keys[6], 71), 0)
    key = draw_key(jax.random.fold_in(keys[6], 71), 0)
    value = bell_draw(keys[2], (FRAMES, HEIGHT, WIDTH, CHANNELS), 1.0, 6.0, ((0, 64), (1, 2), (2, 8)))
    out_grad = bell_draw(keys[3], (FRAMES, HEIGHT, WIDTH, CHANNELS), 1.0, 6.0, ((0, 64), (1, 2), (2, 8)))
    tile_window = place_ends((jax.random.randint(keys[4], (PERIODS, 2, 9), 0, 4) < 3).astype(jnp.int32), jax.random.fold_in(keys[4], 1), 0, 1)
    period_link = draw_period_link(jax.random.fold_in(keys[6], 71), 0)
    return {"query": query, "key": key, "value": value, "out_grad": out_grad, "tile_window": tile_window, "period_link": period_link}


NEG_FILL = -1e+30

def to_tiles(array):
    count = array.shape[0]
    channels = array.shape[-1]
    blocks_rows = array.shape[1] // S
    blocks_cols = array.shape[2] // S
    shaped = array.reshape(count, blocks_rows, S, blocks_cols, S, channels).transpose(0, 1, 3, 2, 4, 5)
    return shaped.reshape(count, blocks_rows, blocks_cols, S * S, channels)

def from_tiles(array):
    count, blocks_rows, blocks_cols, cells, channels = array.shape
    shaped = array.reshape(count, blocks_rows, blocks_cols, S, S, channels).transpose(0, 1, 3, 2, 4, 5)
    return shaped.reshape(count, blocks_rows * S, blocks_cols * S, channels)

def neighbours(array):
    blocks_rows, blocks_cols = (array.shape[1], array.shape[2])
    padded = jnp.pad(array, ((0, 0), (1, 1), (1, 1), (0, 0), (0, 0)))
    pieces = [padded[:, 1 + row_step:1 + row_step + blocks_rows, 1 + col_step:1 + col_step + blocks_cols] for row_step in (-1, 0, 1) for col_step in (-1, 0, 1)]
    return jnp.stack(pieces, axis=3)

def fold_back(array):
    count, blocks_rows, blocks_cols = (array.shape[0], array.shape[1], array.shape[2])
    summed = jnp.zeros((count, blocks_rows + 2, blocks_cols + 2) + array.shape[4:], jnp.float32)
    position = 0
    for row_step in (-1, 0, 1):
        for col_step in (-1, 0, 1):
            summed = summed.at[:, 1 + row_step:1 + row_step + blocks_rows, 1 + col_step:1 + col_step + blocks_cols].add(array[:, :, :, position])
            position = position + 1
    return summed[:, 1:-1, 1:-1]

def split_heads(array):
    return array.reshape(array.shape[:-1] + (HEADS, HD))

def barrier_round(array):
    return lax.optimization_barrier(array.astype(jnp.bfloat16)).astype(jnp.float32)

def reference(query, key, value, out_grad, tile_window, period_link):
    periods = FRAMES // FR
    blocks_rows = HEIGHT // S
    blocks_cols = WIDTH // S
    scale = 1.0 / math.sqrt(HD)
    row_steps = jnp.array([-1, -1, -1, 0, 0, 0, 1, 1, 1], jnp.int32)
    col_steps = jnp.array([-1, 0, 1, -1, 0, 1, -1, 0, 1], jnp.int32)
    rows_in = jnp.arange(blocks_rows, dtype=jnp.int32)[:, None, None] + row_steps[None, None, :]
    cols_in = jnp.arange(blocks_cols, dtype=jnp.int32)[None, :, None] + col_steps[None, None, :]
    inside = ((rows_in >= 0) & (rows_in < blocks_rows) & (cols_in >= 0) & (cols_in < blocks_cols)).astype(jnp.float32)
    center = (jnp.arange(9) == 4).astype(jnp.float32)

    def take(array, first):
        return lax.dynamic_slice_in_dim(array, first, FR, 0)

    def step(carry, period):
        carry_keys, carry_values = carry
        start = (period * FR).astype(jnp.int32)
        back = (jnp.maximum(period - 1, 0) * FR).astype(jnp.int32)
        queries = split_heads(to_tiles(take(query, start))).astype(jnp.float32)
        grads = split_heads(to_tiles(take(out_grad, start))).astype(jnp.float32)
        key_window = split_heads(neighbours(to_tiles(jnp.concatenate([take(key, back), take(key, start)], 0)))).astype(jnp.float32)
        value_window = split_heads(neighbours(to_tiles(jnp.concatenate([take(value, back), take(value, start)], 0)))).astype(jnp.float32)
        window = lax.dynamic_index_in_dim(tile_window, period, 0, keepdims=False).astype(jnp.float32)
        link = lax.dynamic_index_in_dim(period_link, period, 0, keepdims=False).astype(jnp.float32)
        back_ok = link * (period > 0).astype(jnp.float32)
        rows = jnp.stack([window[0] * back_ok, jnp.maximum(window[1], center)])
        allow = jnp.repeat(rows, FR, axis=0)[:, None, None, :] * inside[None]
        mask = jnp.transpose(allow, (1, 2, 0, 3))[:, :, None, None, None, :, :, None] > 0.5
        scores = jnp.einsum('fabihd,tabojhd->abhfitoj', queries, key_window) * scale
        peak = lax.optimization_barrier(jnp.max(jnp.where(mask, scores, NEG_FILL), axis=(5, 6, 7), keepdims=True))
        total = lax.optimization_barrier(jnp.sum(jnp.where(mask, jnp.exp(scores - peak), 0.0), axis=(5, 6, 7), keepdims=True))
        log_total = peak + jnp.log(total)
        weights = jnp.where(mask, jnp.exp(scores - log_total), 0.0)
        rounded = barrier_round(weights)
        attended = jnp.einsum('abhfitoj,tabojhd->fabihd', rounded, value_window)
        out_round = barrier_round(attended)
        delta = lax.optimization_barrier(jnp.sum(grads * out_round, axis=-1))
        delta_wide = jnp.transpose(delta, (1, 2, 4, 0, 3))[:, :, :, :, :, None, None, None]
        grad_weights = jnp.einsum('fabihd,tabojhd->abhfitoj', grads, value_window)
        grad_scores = barrier_round(weights * (grad_weights - delta_wide))
        query_part = jnp.einsum('abhfitoj,tabojhd->fabihd', grad_scores, key_window) * scale
        key_part = fold_back(jnp.einsum('abhfitoj,fabihd->tabojhd', grad_scores, queries).reshape(2 * FR, blocks_rows, blocks_cols, 9, S * S, HEADS * HD))
        value_part = fold_back(jnp.einsum('abhfitoj,fabihd->tabojhd', rounded, grads).reshape(2 * FR, blocks_rows, blocks_cols, 9, S * S, HEADS * HD))
        emit_keys = ((carry_keys + key_part[:FR]) * scale).astype(jnp.bfloat16)
        emit_values = (carry_values + value_part[:FR]).astype(jnp.bfloat16)
        flat_shape = (FR, blocks_rows, blocks_cols, S * S, HEADS * HD)
        outputs = (out_round.reshape(flat_shape).astype(jnp.bfloat16), query_part.reshape(flat_shape).astype(jnp.bfloat16), emit_keys, emit_values)
        return ((key_part[FR:], value_part[FR:]), outputs)
    zeros = jnp.zeros((FR, blocks_rows, blocks_cols, S * S, HEADS * HD), jnp.float32)
    carry, outputs = lax.scan(step, (zeros, zeros), jnp.arange(periods, dtype=jnp.int32))
    attn_tiles, query_tiles, key_tiles, value_tiles = outputs
    key_tiles = jnp.concatenate([key_tiles[1:], (carry[0] * scale).astype(jnp.bfloat16)[None]], 0)
    value_tiles = jnp.concatenate([value_tiles[1:], carry[1].astype(jnp.bfloat16)[None]], 0)

    def whole(tiles):
        return from_tiles(tiles.reshape((FRAMES,) + tiles.shape[2:]))
    return (whole(attn_tiles), whole(query_tiles), whole(key_tiles), whole(value_tiles))
```

```python
import functools
import math

import jax
import jax.numpy as jnp
from jax import lax
from jax.experimental import pallas as pl
from jax.experimental.pallas import tpu as pltpu
from jax.sharding import PartitionSpec as P

HD = 128
S = 4
ROWS = 8
COLS = 16
OWN = ROWS * COLS
HALF = S * COLS
EDGE = ROWS * S
CORNER = S * S
SIDE = EDGE + CORNER
AREA = OWN + HALF + 2 * SIDE
R_AT = OWN
L_AT = OWN + HALF
E_AT = L_AT + SIDE
NEG = -1e30
MESH = pl.DeviceIdType.MESH
F32 = jnp.float32
BF16 = jnp.bfloat16

COMPUTE = True
RELAY = True
UNROLL = 1


def nt(a, b):
    return lax.dot_general(a, b, (((1,), (1,)), ((), ())), preferred_element_type=F32)


def nn(a, b):
    return lax.dot_general(a, b, (((1,), (0,)), ((), ())), preferred_element_type=F32)


def edge_pick(rows):
    count = rows * S
    out = lax.broadcasted_iota(jnp.int32, (2 * count, rows * COLS), 0)
    src = lax.broadcasted_iota(jnp.int32, (2 * count, rows * COLS), 1)
    right = (out >= count).astype(jnp.int32)
    place = out - right * count
    want = lax.shift_right_logical(place, 2) * COLS + lax.bitwise_and(place, 3) + right * (COLS - S)
    return jnp.where(src == want, 1.0, 0.0).astype(BF16)


def kernel(
    window, link, q_ref, k_ref, v_ref, g_ref, o_ref, dq_ref, dk_ref, dv_ref,
    kv, qg, stats, relay, pack_own, pack_r, pack_t, pack_tr, spack, sown, bias_f, bias_b, stat_rows,
    send, recv, relay_send, relay_recv, ssend, srecv, *, heads, periods, n_cols,
):
    channels = heads * HD
    scale = 1.0 / math.sqrt(HD)
    p = lax.axis_index("tm")
    r = lax.axis_index("row")
    c = lax.axis_index("col")
    nxt = lax.rem(p + 1, periods)
    prv = lax.rem(p + periods - 1, periods)
    mate = 1 - r
    left = lax.rem(c + n_cols - 1, n_cols)
    right = lax.rem(c + 1, n_cols)
    y_lo = lax.rem(p // 2, 4)
    high = y_lo // 2
    far = p + 4 - 8 * high
    ahead = r + high - 2 * r * high
    behind = 1 - ahead

    barrier = pltpu.get_barrier_semaphore()
    friends = [
        (t, row, col)
        for t in (p, prv, nxt)
        for row in (r, mate)
        for col in (c, left, right)
        if not (t is p and row is r and col is c)
    ]
    if RELAY:
        friends += [(far, r, c), (far, mate, c)]
    for friend in friends:
        pl.semaphore_signal(barrier, inc=1, device_id=friend, device_id_type=MESH)

    kv[:OWN, :channels] = k_ref[...]
    kv[:OWN, channels:] = v_ref[...]
    qg[:OWN, :channels] = q_ref[...]
    qg[:OWN, channels:] = g_ref[...]
    half_at = pl.multiple_of(HALF * (1 - r), HALF)
    pl.semaphore_wait(barrier, len(friends))

    bufs = (kv, qg)
    toward = (nxt, prv)
    pending = []

    def copy(src, dst, a, b, i, device):
        return pltpu.make_async_remote_copy(
            src_ref=src, dst_ref=dst, send_sem=a.at[i], recv_sem=b.at[i],
            device_id=device, device_id_type=MESH,
        )

    def go(x, slot, src, at, size, device):
        op = copy(src, bufs[x].at[pl.ds(at, size)], send, recv, x * 11 + slot, device)
        op.start()
        pending.append(op)
        return op

    got = {}

    def begin(x):
        buf = bufs[x]
        t = toward[x]
        if RELAY:
            for way in range(2):
                op = copy(
                    buf.at[pl.ds(pl.multiple_of(half_at + way * (HALF // 2), HALF // 2), HALF // 2)],
                    relay.at[x, way], relay_send, relay_recv, x * 4 + way,
                    (far, ahead if way == 0 else behind, c),
                )
                op.start()
                pending.append(op)
                got[x, "hop", way] = op
        else:
            got[x, "r"] = go(x, 0, buf.at[pl.ds(half_at, HALF)], R_AT, HALF, (p, mate, c))
        got[x, "t"] = go(x, 1, buf.at[pl.ds(0, OWN)], AREA, OWN, (t, r, c))
        pack_own[x] = nn(edge_pick(ROWS), buf[:OWN, :]).astype(BF16)
        got[x, "le"] = go(x, 2, pack_own.at[x, pl.ds(0, EDGE)], E_AT, EDGE, (p, r, left))
        got[x, "re"] = go(x, 3, pack_own.at[x, pl.ds(EDGE, EDGE)], L_AT, EDGE, (p, r, right))

    def hop(x):
        if RELAY:
            for way in range(2):
                got[x, "hop", way].wait_recv()
                op = copy(
                    relay.at[x, way],
                    bufs[x].at[pl.ds(R_AT + way * (HALF // 2), HALF // 2)],
                    relay_send, relay_recv, x * 4 + 2 + way,
                    (far, ahead if way == 0 else behind, c),
                )
                op.start()
                pending.append(op)
                got[x, "r", way] = op

    def after_r(x):
        buf = bufs[x]
        if RELAY:
            for way in range(2):
                got[x, "r", way].wait_recv()
        else:
            got[x, "r"].wait_recv()
        got[x, "tr"] = go(x, 4, buf.at[pl.ds(R_AT, HALF)], AREA + R_AT, HALF, (toward[x], r, c))
        pack_r[x] = nn(edge_pick(S), buf[R_AT:L_AT, :]).astype(BF16)
        got[x, "lc"] = go(x, 5, pack_r.at[x, pl.ds(0, CORNER)], E_AT + EDGE, CORNER, (p, r, left))
        got[x, "rc"] = go(x, 6, pack_r.at[x, pl.ds(CORNER, CORNER)], L_AT + EDGE, CORNER, (p, r, right))

    def after_t(x):
        buf = bufs[x]
        got[x, "t"].wait_recv()
        pack_t[x] = nn(edge_pick(ROWS), buf[AREA:AREA + OWN, :]).astype(BF16)
        got[x, "tle"] = go(x, 7, pack_t.at[x, pl.ds(0, EDGE)], AREA + E_AT, EDGE, (p, r, left))
        got[x, "tre"] = go(x, 8, pack_t.at[x, pl.ds(EDGE, EDGE)], AREA + L_AT, EDGE, (p, r, right))

    def after_tr(x):
        buf = bufs[x]
        got[x, "tr"].wait_recv()
        pack_tr[x] = nn(edge_pick(S), buf[AREA + R_AT:AREA + L_AT, :]).astype(BF16)
        got[x, "tlc"] = go(x, 9, pack_tr.at[x, pl.ds(0, CORNER)], AREA + E_AT + EDGE, CORNER, (p, r, left))
        got[x, "trc"] = go(x, 10, pack_tr.at[x, pl.ds(CORNER, CORNER)], AREA + L_AT + EDGE, CORNER, (p, r, right))

    def finish(x):
        for name in ("le", "re", "lc", "rc", "tle", "tre", "tlc", "trc"):
            got[x, name].wait_recv()

    begin(0)
    begin(1)

    token = lax.broadcasted_iota(jnp.int32, (OWN, 1), 0)
    own_row = lax.shift_right_logical(token, 6)
    own_col = lax.bitwise_and(lax.shift_right_logical(token, 2), 3)
    place = lax.broadcasted_iota(jnp.int32, (1, 2 * AREA), 1)
    second = place >= AREA
    j = jnp.where(second, place - AREA, place)
    r_row = 2 - 3 * r
    side = jnp.where(j >= E_AT, j - E_AT, j - L_AT)
    side_row = jnp.where(side >= EDGE, r_row, lax.shift_right_arithmetic(side, 4))
    area_row = jnp.where(
        j >= L_AT, side_row, jnp.where(j >= R_AT, r_row, lax.shift_right_logical(j, 6))
    )
    area_col = jnp.where(
        j >= E_AT, 4,
        jnp.where(j >= L_AT, -1, lax.bitwise_and(lax.shift_right_logical(j, 2), 3)),
    )
    whole_col = area_col + 4 * c
    inside = (whole_col >= 0) & (whole_col < 4 * n_cols)
    dr = area_row - own_row
    dc = area_col - own_col
    near = (dr >= -1) & (dr <= 1) & (dc >= -1) & (dc <= 1) & inside
    code = jnp.where(near, 3 * dr + dc + 4, -1)
    later = jnp.minimum(p + 1, periods - 1)
    back_ok = link[p] * (p > 0).astype(jnp.int32)
    ahead_ok = link[later] * (p + 1 < periods).astype(jnp.int32)
    allow_f = jnp.zeros((OWN, 2 * AREA), jnp.int32)
    allow_b = jnp.zeros((OWN, 2 * AREA), jnp.int32)
    for o in range(9):
        own_ok = 1 if o == 4 else window[p, 1, o]
        at = code == o
        allow_f = jnp.where(at, jnp.where(second, window[p, 0, o] * back_ok, own_ok), allow_f)
        at = code == 8 - o
        allow_b = jnp.where(at, jnp.where(second, window[later, 0, o] * ahead_ok, own_ok), allow_b)
    bias_f[...] = jnp.where(allow_f > 0, 0.0, NEG)
    bias_b[...] = jnp.where(allow_b > 0, 0.0, NEG)

    hop(0)
    hop(1)
    after_t(0)
    after_r(0)
    after_t(1)
    after_tr(0)
    after_r(1)
    finish(0)

    lane = lax.broadcasted_iota(jnp.int32, (OWN, 128), 1)
    lane16 = lax.bitwise_and(lane, 15)

    def forward(h, acc):
        ch = pl.ds(pl.multiple_of(h * HD, HD), HD)
        vh = pl.ds(pl.multiple_of(channels + h * HD, HD), HD)
        scores = nt(qg[:OWN, ch], kv[:, ch]) * scale + bias_f[...]
        peak = jnp.max(scores, axis=1, keepdims=True)
        e = jnp.exp(scores - peak)
        total = jnp.sum(e, axis=1, keepdims=True)
        weights = e * (1.0 / total)
        out = nn(weights.astype(BF16), kv[:, vh]).astype(BF16)
        o_ref[:, ch] = out
        g = qg[:OWN, vh]
        delta = jnp.sum(g.astype(F32) * out.astype(F32), axis=1, keepdims=True)
        ds = (weights * (nt(g, kv[:, vh]) - delta)).astype(BF16)
        dq_ref[:, ch] = (nn(ds, kv[:, ch]) * scale).astype(BF16)
        acc = jnp.where(lane16 == h, peak + jnp.log(total), acc)
        return jnp.where(lane16 == h + heads, delta, acc)

    acc = jnp.zeros((OWN, 128), F32)
    if COMPUTE:
        acc = lax.fori_loop(0, heads, forward, acc, unroll=UNROLL)
    hi = acc.astype(BF16).astype(F32)
    mid = (acc - hi).astype(BF16).astype(F32)
    low = acc - hi - mid
    parts = jnp.where(lane < 16, hi, jnp.where(lane < 32, mid, low)).astype(BF16)
    sown[...] = parts
    stats[:OWN, :] = parts
    spack[...] = nn(edge_pick(ROWS), parts).astype(BF16)
    corner_at = pl.multiple_of(CORNER * (1 - r), CORNER)
    sops = []

    def stat(src, at, size, device):
        i = len(sops)
        op = copy(src, stats.at[pl.ds(at, size)], ssend, srecv, i, device)
        op.start()
        sops.append(op)

    for base, t in ((AREA, prv), (0, p)):
        stat(sown.at[pl.ds(half_at, HALF)], base + R_AT, HALF, (t, mate, c))
        stat(spack.at[pl.ds(corner_at, CORNER)], base + E_AT + EDGE, CORNER, (t, mate, left))
        stat(
            spack.at[pl.ds(pl.multiple_of(EDGE + corner_at, CORNER), CORNER)],
            base + L_AT + EDGE, CORNER, (t, mate, right),
        )
        stat(spack.at[pl.ds(0, EDGE)], base + E_AT, EDGE, (t, r, left))
        stat(spack.at[pl.ds(EDGE, EDGE)], base + L_AT, EDGE, (t, r, right))
        if base:
            stat(sown, base, OWN, (t, r, c))

    after_tr(1)
    finish(1)
    for op in sops:
        op.wait_recv()
    pick_row = lax.broadcasted_iota(jnp.int32, (16, 128), 0)
    pick_lane = lax.broadcasted_iota(jnp.int32, (16, 128), 1)
    pick = jnp.where((lax.bitwise_and(pick_lane, 15) == pick_row) & (pick_lane < 48), 1.0, 0.0)
    stat_rows[...] = nt(pick.astype(BF16), stats[...])

    def backward(h, carry):
        ch = pl.ds(pl.multiple_of(h * HD, HD), HD)
        vh = pl.ds(pl.multiple_of(channels + h * HD, HD), HD)
        scores = nt(kv[:OWN, ch], qg[:, ch]) * scale + bias_b[...]
        weights = jnp.exp(scores - stat_rows[pl.ds(h, 1), :])
        dv_ref[:, ch] = nn(weights.astype(BF16), qg[:, vh]).astype(BF16)
        dp = nt(kv[:OWN, vh], qg[:, vh])
        ds = (weights * (dp - stat_rows[pl.ds(h + heads, 1), :])).astype(BF16)
        dk_ref[:, ch] = (nn(ds, qg[:, ch]) * scale).astype(BF16)
        return carry

    if COMPUTE:
        lax.fori_loop(0, heads, backward, 0, unroll=UNROLL)
    for op in pending + sops:
        op.wait_send()


def body(query, key, value, out_grad, tile_window, period_link):
    channels = query.shape[-1]
    heads = channels // HD
    flat = [x.reshape(OWN, channels) for x in (query, key, value, out_grad)]
    whole = pl.BlockSpec(memory_space=pltpu.VMEM)
    table = pl.BlockSpec(memory_space=pltpu.SMEM)
    outs = pl.pallas_call(
        functools.partial(
            kernel, heads=heads, periods=lax.axis_size("tm"), n_cols=lax.axis_size("col")
        ),
        out_shape=[jax.ShapeDtypeStruct((OWN, channels), BF16)] * 4,
        in_specs=[table, table] + [whole] * 4,
        out_specs=[whole] * 4,
        scratch_shapes=[
            pltpu.VMEM((2 * AREA, 2 * channels), BF16),
            pltpu.VMEM((2 * AREA, 2 * channels), BF16),
            pltpu.VMEM((2 * AREA, 128), BF16),
            pltpu.VMEM((2, 2, HALF // 2, 2 * channels), BF16),
            pltpu.VMEM((2, 2 * EDGE, 2 * channels), BF16),
            pltpu.VMEM((2, 2 * CORNER, 2 * channels), BF16),
            pltpu.VMEM((2, 2 * EDGE, 2 * channels), BF16),
            pltpu.VMEM((2, 2 * CORNER, 2 * channels), BF16),
            pltpu.VMEM((2 * EDGE, 128), BF16),
            pltpu.VMEM((OWN, 128), BF16),
            pltpu.VMEM((OWN, 2 * AREA), F32),
            pltpu.VMEM((OWN, 2 * AREA), F32),
            pltpu.VMEM((2 * heads, 2 * AREA), F32),
            pltpu.SemaphoreType.DMA((22,)),
            pltpu.SemaphoreType.DMA((22,)),
            pltpu.SemaphoreType.DMA((8,)),
            pltpu.SemaphoreType.DMA((8,)),
            pltpu.SemaphoreType.DMA((11,)),
            pltpu.SemaphoreType.DMA((11,)),
        ],
        compiler_params=pltpu.CompilerParams(
            collective_id=0, has_side_effects=True, vmem_limit_bytes=48 * 1024 * 1024
        ),
    )(tile_window, period_link, *flat)
    return tuple(x.reshape(query.shape) for x in outs)


def solution(mesh):
    spread = P("tm", "row", "col", None)
    return jax.shard_map(
        body,
        mesh=mesh,
        in_specs=(spread, spread, spread, spread, P(), P()),
        out_specs=(spread, spread, spread, spread),
        check_vma=False,
    )
```

```python
import functools
import math

import jax
import jax.numpy as jnp
from jax import lax
from jax.experimental import pallas as pl
from jax.experimental.pallas import tpu as pltpu
from jax.sharding import PartitionSpec as P

HD = 128
S = 4
ROWS = 8
COLS = 16
OWN = ROWS * COLS
HALF = S * COLS
EDGE = ROWS * S
CORNER = S * S
SIDE = EDGE + CORNER
AREA = OWN + HALF + 2 * SIDE
R_AT = OWN
L_AT = OWN + HALF
E_AT = L_AT + SIDE
NEG = -1e30
MESH = pl.DeviceIdType.MESH
F32 = jnp.float32
BF16 = jnp.bfloat16

UNROLL = 8
MAIN = AREA + OWN
REST = 2 * AREA - MAIN
PLAN = (
    "load0", "R0", "T0", "E0", "load1", "mask", "sent0", "R1", "T1", "E1", "t0", "r0", "tr0",
    "near0", "far0", "F", "stat", "r1", "t1", "near1", "B1", "tr1", "far1", "B2",
)


def nt(a, b):
    return lax.dot_general(a, b, (((1,), (1,)), ((), ())), preferred_element_type=F32)


def nn(a, b):
    return lax.dot_general(a, b, (((1,), (0,)), ((), ())), preferred_element_type=F32)


def edge_pick(rows):
    count = rows * S
    out = lax.broadcasted_iota(jnp.int32, (2 * count, rows * COLS), 0)
    src = lax.broadcasted_iota(jnp.int32, (2 * count, rows * COLS), 1)
    right = (out >= count).astype(jnp.int32)
    place = out - right * count
    want = lax.shift_right_logical(place, 2) * COLS + lax.bitwise_and(place, 3) + right * (COLS - S)
    return jnp.where(src == want, 1.0, 0.0).astype(BF16)


def kernel(
    window, link, q_ref, k_ref, v_ref, g_ref, o_out, dq_out, dk_out, dv_out,
    kv, qg, stats, pack_own, pack_r, pack_t, pack_tr, spack, sown, bias_f, bias_b, bias_rest,
    stat_rows, o_ref, dq_ref, dk_ref, dv_ref, dk_sum, dv_sum,
    local, send, recv, ssend, srecv, *, heads, periods, n_cols,
):
    channels = heads * HD
    scale = 1.0 / math.sqrt(HD)
    p = lax.axis_index("tm")
    r = lax.axis_index("row")
    c = lax.axis_index("col")
    nxt = lax.rem(p + 1, periods)
    prv = lax.rem(p + periods - 1, periods)
    mate = 1 - r
    has_left = c > 0
    has_right = c < n_cols - 1
    left = jnp.maximum(c - 1, 0)
    right = jnp.minimum(c + 1, n_cols - 1)
    bufs = (kv, qg)
    toward = (nxt, prv)

    loads = []
    for i, (src, buf, at) in enumerate(
        ((k_ref, kv, 0), (v_ref, kv, channels), (q_ref, qg, 0), (g_ref, qg, channels))
    ):
        op = pltpu.make_async_copy(src, buf.at[pl.ds(0, OWN), pl.ds(at, channels)], local.at[i])
        op.start()
        loads.append(op)

    barrier = pltpu.get_barrier_semaphore()

    def greet(*friends):
        for friend in friends:
            pl.semaphore_signal(barrier, inc=1, device_id=friend, device_id_type=MESH)

    greet((p, mate, c), (nxt, r, c), (prv, r, c), (nxt, mate, c), (prv, mate, c))

    @pl.when(has_left)
    def _():
        greet(*[(t, row, left) for t in (p, nxt, prv) for row in (r, mate)])

    @pl.when(has_right)
    def _():
        greet(*[(t, row, right) for t in (p, nxt, prv) for row in (r, mate)])

    both = 5 + 6 * has_left.astype(jnp.int32) + 6 * has_right.astype(jnp.int32)
    pl.semaphore_wait(barrier, both)

    for missing, at in ((has_left, L_AT), (has_right, E_AT)):

        @pl.when(jnp.logical_not(missing))
        def _():
            for base in (0, AREA):
                for buf in (kv, qg):
                    buf[pl.ds(base + at, SIDE), :] = jnp.zeros((SIDE, 2 * channels), BF16)
                stats[pl.ds(base + at, SIDE), :] = jnp.zeros((SIDE, 128), BF16)

    half_at = pl.multiple_of(HALF * (1 - r), HALF)
    corner_at = pl.multiple_of(CORNER * (1 - r), CORNER)
    NAMES = ("R", "T", "TR", "le", "re", "lc", "rc", "tle", "tre", "tlc", "trc")
    pending, lefts, rights = [], [], []

    def copy(src, dst, a, b, i, device):
        return pltpu.make_async_remote_copy(
            src_ref=src, dst_ref=dst, send_sem=a.at[i], recv_sem=b.at[i],
            device_id=device, device_id_type=MESH,
        )

    got = {}

    def make(x, name, src, at, size, device):
        op = copy(src, bufs[x].at[pl.ds(at, size)], send, recv, x * 11 + NAMES.index(name), device)
        got[name, x] = op
        return op

    def go(*args):
        op = make(*args)
        op.start()
        pending.append(op)

    def sides(x, tag, pack, rows, base, shift):
        count = rows * S
        a = make(x, tag[0], pack.at[x, pl.ds(0, count)], base + E_AT + shift, count, (p, r, left))
        b = make(x, tag[1], pack.at[x, pl.ds(count, count)], base + L_AT + shift, count, (p, r, right))
        pl.when(has_left)(a.start)
        pl.when(has_right)(b.start)
        lefts.append(a)
        rights.append(b)

    def begin_r(x):
        go(x, "R", bufs[x].at[pl.ds(half_at, HALF)], R_AT, HALF, (p, mate, c))

    def begin_t(x):
        go(x, "T", bufs[x].at[pl.ds(0, OWN)], AREA, OWN, (toward[x], r, c))

    def begin_e(x):
        pack_own[x] = nn(edge_pick(ROWS), bufs[x][:OWN, :]).astype(BF16)
        sides(x, ("le", "re"), pack_own, ROWS, 0, 0)

    def after_r(x):
        got["R", x].wait_recv()
        turn = lax.rem(p, 8) == (7 if x == 0 else 0)
        at = pl.multiple_of(jnp.where(turn, half_at, R_AT), HALF)
        row = jnp.where(turn, mate, r)
        go(x, "TR", bufs[x].at[pl.ds(at, HALF)], AREA + R_AT, HALF, (toward[x], row, c))
        pack_r[x] = nn(edge_pick(S), bufs[x][R_AT:L_AT, :]).astype(BF16)
        sides(x, ("lc", "rc"), pack_r, S, 0, EDGE)

    def after_t(x):
        got["T", x].wait_recv()
        pack_t[x] = nn(edge_pick(ROWS), bufs[x][AREA:AREA + OWN, :]).astype(BF16)
        sides(x, ("tle", "tre"), pack_t, ROWS, AREA, 0)

    def after_tr(x):
        got["TR", x].wait_recv()
        pack_tr[x] = nn(edge_pick(S), bufs[x][AREA + R_AT:AREA + L_AT, :]).astype(BF16)
        sides(x, ("tlc", "trc"), pack_tr, S, AREA, EDGE)

    def arrived(x, from_right, from_left):
        @pl.when(has_right)
        def _():
            for name in from_right:
                got[name, x].wait_recv()

        @pl.when(has_left)
        def _():
            for name in from_left:
                got[name, x].wait_recv()

    def near(x):
        arrived(x, ("le", "lc"), ("re", "rc"))

    def far(x):
        arrived(x, ("tle", "tlc"), ("tre", "trc"))

    def codes(first, count):
        token = lax.broadcasted_iota(jnp.int32, (OWN, 1), 0)
        own_row = lax.shift_right_logical(token, 6)
        own_col = lax.bitwise_and(lax.shift_right_logical(token, 2), 3)
        place = lax.broadcasted_iota(jnp.int32, (1, count), 1) + first
        second = place >= AREA
        j = jnp.where(second, place - AREA, place)
        r_row = 2 - 3 * r
        side = jnp.where(j >= E_AT, j - E_AT, j - L_AT)
        side_row = jnp.where(side >= EDGE, r_row, lax.shift_right_arithmetic(side, 4))
        area_row = jnp.where(
            j >= L_AT, side_row, jnp.where(j >= R_AT, r_row, lax.shift_right_logical(j, 6))
        )
        area_col = jnp.where(
            j >= E_AT, 4,
            jnp.where(j >= L_AT, -1, lax.bitwise_and(lax.shift_right_logical(j, 2), 3)),
        )
        whole_col = area_col + 4 * c
        inside = (whole_col >= 0) & (whole_col < 4 * n_cols)
        dr = area_row - own_row
        dc = area_col - own_col
        close = (dr >= -1) & (dr <= 1) & (dc >= -1) & (dc <= 1) & inside
        return jnp.where(close, 3 * dr + dc + 4, -1), second

    def bias(first, count, source, ok, turned):
        code, second = codes(first, count)
        allow = jnp.zeros((OWN, count), jnp.int32)
        for o in range(9):
            own_ok = 1 if o == 4 else window[o, 1, p]
            entry = jnp.where(second, window[o, 0, source] * ok, own_ok)
            allow = jnp.where(code == (8 - o if turned else o), entry, allow)
        return jnp.where(allow > 0, 0.0, NEG)

    def masks():
        later = jnp.minimum(p + 1, periods - 1)
        back_ok = link[p] * (p > 0).astype(jnp.int32)
        ahead_ok = link[later] * (p + 1 < periods).astype(jnp.int32)
        bias_f[...] = bias(0, 2 * AREA, p, back_ok, False)
        bias_b[...] = bias(0, MAIN, later, ahead_ok, True)
        bias_rest[...] = bias(MAIN, REST, later, ahead_ok, True)

    lane = lax.broadcasted_iota(jnp.int32, (OWN, 128), 1)
    lane16 = lax.bitwise_and(lane, 15)

    def forward(h, total_stats):
        ch = pl.ds(pl.multiple_of(h * HD, HD), HD)
        vh = pl.ds(pl.multiple_of(channels + h * HD, HD), HD)
        scores = nt(qg[:OWN, ch], kv[:, ch]) * scale + bias_f[...]
        peak = jnp.max(scores, axis=1, keepdims=True)
        e = jnp.exp(scores - peak)
        total = jnp.sum(e, axis=1, keepdims=True)
        weights = e * (1.0 / total)
        out = nn(weights.astype(BF16), kv[:, vh]).astype(BF16)
        o_ref[:, ch] = out
        g = qg[:OWN, vh]
        delta = jnp.sum(g.astype(F32) * out.astype(F32), axis=1, keepdims=True)
        ds = (weights * (nt(g, kv[:, vh]) - delta)).astype(BF16)
        dq_ref[:, ch] = (nn(ds, kv[:, ch]) * scale).astype(BF16)
        total_stats = jnp.where(lane16 == h, peak + jnp.log(total), total_stats)
        return jnp.where(lane16 == h + heads, delta, total_stats)

    saves = []

    def save(pairs):
        for src, dst in pairs:
            op = pltpu.make_async_copy(src, dst, local.at[4 + len(saves)])
            op.start()
            saves.append(op)

    result = []

    def run_forward():
        zero = jnp.zeros((OWN, 128), F32)
        result.append(lax.fori_loop(0, heads, forward, zero, unroll=UNROLL))

    sops, slefts, srights = [], [], []

    def send_stats():
        value = result[0]
        hi = value.astype(BF16).astype(F32)
        mid = (value - hi).astype(BF16).astype(F32)
        low = value - hi - mid
        parts = jnp.where(lane < 16, hi, jnp.where(lane < 32, mid, low)).astype(BF16)
        sown[...] = parts
        stats[:OWN, :] = parts
        spack[...] = nn(edge_pick(ROWS), parts).astype(BF16)

        def stat(kept, src, at, size, device):
            i = len(sops) + len(slefts) + len(srights)
            op = copy(src, stats.at[pl.ds(at, size)], ssend, srecv, i, device)
            kept.append(op)

        right_corner = pl.multiple_of(EDGE + corner_at, CORNER)
        for base, t in ((0, p), (AREA, prv)):
            stat(sops, sown.at[pl.ds(half_at, HALF)], base + R_AT, HALF, (t, mate, c))
            stat(slefts, spack.at[pl.ds(corner_at, CORNER)], base + E_AT + EDGE, CORNER, (t, mate, left))
            stat(srights, spack.at[pl.ds(right_corner, CORNER)], base + L_AT + EDGE, CORNER, (t, mate, right))
            stat(slefts, spack.at[pl.ds(0, EDGE)], base + E_AT, EDGE, (t, r, left))
            stat(srights, spack.at[pl.ds(EDGE, EDGE)], base + L_AT, EDGE, (t, r, right))
        stat(sops, sown, AREA, OWN, (prv, r, c))
        for op in sops:
            op.start()

        @pl.when(has_left)
        def _():
            for op in slefts:
                op.start()

        @pl.when(has_right)
        def _():
            for op in srights:
                op.start()

        save(((o_ref, o_out), (dq_ref, dq_out)))

    def rows():
        for op in sops:
            op.wait_recv()

        @pl.when(has_right)
        def _():
            for op in slefts:
                op.wait_recv()

        @pl.when(has_left)
        def _():
            for op in srights:
                op.wait_recv()

        pick_row = lax.broadcasted_iota(jnp.int32, (16, 128), 0)
        pick_lane = lax.broadcasted_iota(jnp.int32, (16, 128), 1)
        same = lax.bitwise_and(pick_lane, 15) == pick_row
        pick = jnp.where(same & (pick_lane < 48), 1.0, 0.0)
        stat_rows[...] = nt(pick.astype(BF16), stats[:MAIN, :])
        return nt(pick.astype(BF16), stats[MAIN:, :])

    def backward(h, at, count, bias_now, lse, delta):
        ch = pl.ds(pl.multiple_of(h * HD, HD), HD)
        vh = pl.ds(pl.multiple_of(channels + h * HD, HD), HD)
        span = pl.ds(at, count)
        scores = nt(kv[:OWN, ch], qg[span, ch]) * scale + bias_now
        weights = jnp.exp(scores - lse)
        dv = nn(weights.astype(BF16), qg[span, vh])
        dp = nt(kv[:OWN, vh], qg[span, vh])
        ds = (weights * (dp - delta)).astype(BF16)
        return nn(ds, qg[span, ch]), dv

    kept = []

    def main_backward():
        kept.append(rows())

        def one(h, carry):
            ch = pl.ds(pl.multiple_of(h * HD, HD), HD)
            lse = stat_rows[pl.ds(h, 1), :]
            delta = stat_rows[pl.ds(h + heads, 1), :]
            dk, dv = backward(h, 0, MAIN, bias_b[...], lse, delta)
            dk_sum[:, ch] = dk
            dv_sum[:, ch] = dv
            return carry

        lax.fori_loop(0, heads, one, 0, unroll=UNROLL)

    def rest_backward():
        for h in range(heads):
            ch = pl.ds(h * HD, HD)
            lse = kept[0][h:h + 1, :]
            delta = kept[0][h + heads:h + heads + 1, :]
            dk, dv = backward(h, MAIN, REST, bias_rest[...], lse, delta)
            dk_ref[:, ch] = ((dk_sum[:, ch] + dk) * scale).astype(BF16)
            dv_ref[:, ch] = (dv_sum[:, ch] + dv).astype(BF16)
        save(((dk_ref, dk_out), (dv_ref, dv_out)))

    def load(x):
        loads[2 * x].wait()
        loads[2 * x + 1].wait()

    steps = {
        "R": begin_r, "T": begin_t, "E": begin_e, "r": after_r, "t": after_t, "tr": after_tr,
        "near": near, "far": far, "load": load, "sent": lambda x: got["R", x].wait_send(),
    }
    plain = {
        "mask": masks, "F": run_forward, "stat": send_stats, "B1": main_backward, "B2": rest_backward,
    }
    done_sends = []
    for word in PLAN:
        if word in plain:
            plain[word]()
        else:
            steps[word[:-1]](int(word[-1]))
            if word[:-1] == "sent":
                done_sends.append(got["R", int(word[-1])])
    for op in pending + sops:
        if not any(op is one for one in done_sends):
            op.wait_send()

    @pl.when(has_left)
    def _():
        for op in lefts + slefts:
            op.wait_send()

    @pl.when(has_right)
    def _():
        for op in rights + srights:
            op.wait_send()

    for op in saves:
        op.wait()


def flush(*refs):
    count = len(refs) // 2
    ops = [pltpu.make_async_copy(refs[i], refs[count + i], refs[-1].at[i]) for i in range(count)]
    for op in ops:
        op.start()
    for op in ops:
        op.wait()


def body(query, key, value, out_grad, tile_window, period_link):
    channels = query.shape[-1]
    heads = channels // HD
    flat = [x.reshape(OWN, channels) for x in (query, key, value, out_grad)]
    whole = pl.BlockSpec(memory_space=pltpu.HBM)
    shapes = [jax.ShapeDtypeStruct((OWN, channels), BF16)] * 4
    table = pl.BlockSpec(memory_space=pltpu.SMEM)
    outs = pl.pallas_call(
        functools.partial(
            kernel, heads=heads, periods=lax.axis_size("tm"), n_cols=lax.axis_size("col")
        ),
        out_shape=shapes,
        in_specs=[table, table] + [whole] * 4,
        out_specs=[whole] * 4,
        scratch_shapes=[
            pltpu.VMEM((2 * AREA, 2 * channels), BF16),
            pltpu.VMEM((2 * AREA, 2 * channels), BF16),
            pltpu.VMEM((2 * AREA, 128), BF16),
            pltpu.VMEM((2, 2 * EDGE, 2 * channels), BF16),
            pltpu.VMEM((2, 2 * CORNER, 2 * channels), BF16),
            pltpu.VMEM((2, 2 * EDGE, 2 * channels), BF16),
            pltpu.VMEM((2, 2 * CORNER, 2 * channels), BF16),
            pltpu.VMEM((2 * EDGE, 128), BF16),
            pltpu.VMEM((OWN, 128), BF16),
            pltpu.VMEM((OWN, 2 * AREA), F32),
            pltpu.VMEM((OWN, MAIN), F32),
            pltpu.VMEM((OWN, REST), F32),
            pltpu.VMEM((2 * heads, MAIN), F32),
            pltpu.VMEM((OWN, channels), BF16),
            pltpu.VMEM((OWN, channels), BF16),
            pltpu.VMEM((OWN, channels), BF16),
            pltpu.VMEM((OWN, channels), BF16),
            pltpu.VMEM((OWN, channels), F32),
            pltpu.VMEM((OWN, channels), F32),
            pltpu.SemaphoreType.DMA((8,)),
            pltpu.SemaphoreType.DMA((22,)),
            pltpu.SemaphoreType.DMA((22,)),
            pltpu.SemaphoreType.DMA((11,)),
            pltpu.SemaphoreType.DMA((11,)),
        ],
        compiler_params=pltpu.CompilerParams(
            collective_id=0, has_side_effects=True, vmem_limit_bytes=63 * 1024 * 1024
        ),
    )(tile_window.transpose(2, 1, 0), period_link, *flat)
    outs = pl.pallas_call(
        flush,
        out_shape=shapes,
        in_specs=[whole] * 4,
        out_specs=[whole] * 4,
        scratch_shapes=[pltpu.SemaphoreType.DMA((4,))],
        compiler_params=pltpu.CompilerParams(vmem_limit_bytes=63 * 1024 * 1024),
    )(*outs)
    return tuple(x.reshape(query.shape) for x in outs)


def solution(mesh):
    spread = P("tm", "row", "col", None)
    return jax.shard_map(
        body,
        mesh=mesh,
        in_specs=(spread, spread, spread, spread, P(), P()),
        out_specs=(spread, spread, spread, spread),
        check_vma=False,
    )
```

```python
import functools
import math

import jax
import jax.numpy as jnp
from jax import lax
from jax.experimental import pallas as pl
from jax.experimental.pallas import tpu as pltpu
from jax.sharding import PartitionSpec as P

HD = 128
S = 4
ROWS = 8
COLS = 16
OWN = ROWS * COLS
HALF = S * COLS
EDGE = ROWS * S
CORNER = S * S
SIDE = EDGE + CORNER
AREA = OWN + HALF + 2 * SIDE
R_AT = OWN
L_AT = OWN + HALF
E_AT = L_AT + SIDE
NEG = -1e30
MESH = pl.DeviceIdType.MESH
F32 = jnp.float32
BF16 = jnp.bfloat16

UNROLL = 8
MAIN = AREA + OWN
REST = 2 * AREA - MAIN
PLAN = (
    "load0", "R0", "T0", "E0", "load1", "mask", "E1", "r0", "t0", "R1", "tr0", "T1", "near0",
    "far0", "F", "stat", "r1", "t1", "near1", "B1", "tr1", "far1", "B2",
)


def nt(a, b):
    return lax.dot_general(a, b, (((1,), (1,)), ((), ())), preferred_element_type=F32)


def nn(a, b):
    return lax.dot_general(a, b, (((1,), (0,)), ((), ())), preferred_element_type=F32)


def edge_pick(rows):
    count = rows * S
    out = lax.broadcasted_iota(jnp.int32, (2 * count, rows * COLS), 0)
    src = lax.broadcasted_iota(jnp.int32, (2 * count, rows * COLS), 1)
    right = (out >= count).astype(jnp.int32)
    place = out - right * count
    want = lax.shift_right_logical(place, 2) * COLS + lax.bitwise_and(place, 3) + right * (COLS - S)
    return jnp.where(src == want, 1.0, 0.0).astype(BF16)


def kernel(
    window, link, q_ref, k_ref, v_ref, g_ref, o_out, dq_out, dk_out, dv_out,
    kv, qg, stats, pack_own, pack_r, pack_t, pack_tr, spack, sown, bias_f, bias_b, bias_rest,
    stat_rows, o_ref, dq_ref, dk_ref, dv_ref, dk_sum, dv_sum,
    local, send, recv, ssend, srecv, *, heads, periods, n_cols,
):
    channels = heads * HD
    scale = 1.0 / math.sqrt(HD)
    p = lax.axis_index("tm")
    r = lax.axis_index("row")
    c = lax.axis_index("col")
    nxt = lax.rem(p + 1, periods)
    prv = lax.rem(p + periods - 1, periods)
    mate = 1 - r
    has_left = c > 0
    has_right = c < n_cols - 1
    left = jnp.maximum(c - 1, 0)
    right = jnp.minimum(c + 1, n_cols - 1)
    bufs = (kv, qg)
    toward = (nxt, prv)

    loads = []
    for i, (src, buf, at) in enumerate(
        ((k_ref, kv, 0), (v_ref, kv, channels), (q_ref, qg, 0), (g_ref, qg, channels))
    ):
        op = pltpu.make_async_copy(src, buf.at[pl.ds(0, OWN), pl.ds(at, channels)], local.at[i])
        op.start()
        loads.append(op)

    barrier = pltpu.get_barrier_semaphore()

    def greet(*friends):
        for friend in friends:
            pl.semaphore_signal(barrier, inc=1, device_id=friend, device_id_type=MESH)

    greet((p, mate, c), (nxt, r, c), (prv, r, c), (nxt, mate, c), (prv, mate, c))

    @pl.when(has_left)
    def _():
        greet(*[(t, row, left) for t in (p, nxt, prv) for row in (r, mate)])

    @pl.when(has_right)
    def _():
        greet(*[(t, row, right) for t in (p, nxt, prv) for row in (r, mate)])

    both = 5 + 6 * has_left.astype(jnp.int32) + 6 * has_right.astype(jnp.int32)
    pl.semaphore_wait(barrier, both)

    for missing, at in ((has_left, L_AT), (has_right, E_AT)):

        @pl.when(jnp.logical_not(missing))
        def _():
            for base in (0, AREA):
                for buf in (kv, qg):
                    buf[pl.ds(base + at, SIDE), :] = jnp.zeros((SIDE, 2 * channels), BF16)
                stats[pl.ds(base + at, SIDE), :] = jnp.zeros((SIDE, 128), BF16)

    half_at = pl.multiple_of(HALF * (1 - r), HALF)
    corner_at = pl.multiple_of(CORNER * (1 - r), CORNER)
    NAMES = ("R", "T", "TR", "le", "re", "lc", "rc", "tle", "tre", "tlc", "trc")
    pending, lefts, rights = [], [], []

    def copy(src, dst, a, b, i, device):
        return pltpu.make_async_remote_copy(
            src_ref=src, dst_ref=dst, send_sem=a.at[i], recv_sem=b.at[i],
            device_id=device, device_id_type=MESH,
        )

    got = {}

    def make(x, name, src, at, size, device):
        op = copy(src, bufs[x].at[pl.ds(at, size)], send, recv, x * 11 + NAMES.index(name), device)
        got[name, x] = op
        return op

    def go(*args):
        op = make(*args)
        op.start()
        pending.append(op)

    def sides(x, tag, pack, rows, base, shift):
        count = rows * S
        a = make(x, tag[0], pack.at[x, pl.ds(0, count)], base + E_AT + shift, count, (p, r, left))
        b = make(x, tag[1], pack.at[x, pl.ds(count, count)], base + L_AT + shift, count, (p, r, right))
        pl.when(has_left)(a.start)
        pl.when(has_right)(b.start)
        lefts.append(a)
        rights.append(b)

    def begin_r(x):
        go(x, "R", bufs[x].at[pl.ds(half_at, HALF)], R_AT, HALF, (p, mate, c))

    def begin_t(x):
        go(x, "T", bufs[x].at[pl.ds(0, OWN)], AREA, OWN, (toward[x], r, c))

    def begin_e(x):
        pack_own[x] = nn(edge_pick(ROWS), bufs[x][:OWN, :]).astype(BF16)
        sides(x, ("le", "re"), pack_own, ROWS, 0, 0)

    def after_r(x):
        got["R", x].wait_recv()
        turn = lax.rem(p, 8) == (7 if x == 0 else 0)
        at = pl.multiple_of(jnp.where(turn, half_at, R_AT), HALF)
        row = jnp.where(turn, mate, r)
        go(x, "TR", bufs[x].at[pl.ds(at, HALF)], AREA + R_AT, HALF, (toward[x], row, c))
        pack_r[x] = nn(edge_pick(S), bufs[x][R_AT:L_AT, :]).astype(BF16)
        sides(x, ("lc", "rc"), pack_r, S, 0, EDGE)

    def after_t(x):
        got["T", x].wait_recv()
        pack_t[x] = nn(edge_pick(ROWS), bufs[x][AREA:AREA + OWN, :]).astype(BF16)
        sides(x, ("tle", "tre"), pack_t, ROWS, AREA, 0)

    def after_tr(x):
        got["TR", x].wait_recv()
        pack_tr[x] = nn(edge_pick(S), bufs[x][AREA + R_AT:AREA + L_AT, :]).astype(BF16)
        sides(x, ("tlc", "trc"), pack_tr, S, AREA, EDGE)

    def arrived(x, from_right, from_left):
        @pl.when(has_right)
        def _():
            for name in from_right:
                got[name, x].wait_recv()

        @pl.when(has_left)
        def _():
            for name in from_left:
                got[name, x].wait_recv()

    def near(x):
        arrived(x, ("le", "lc"), ("re", "rc"))

    def far(x):
        arrived(x, ("tle", "tlc"), ("tre", "trc"))

    def codes(first, count):
        token = lax.broadcasted_iota(jnp.int32, (OWN, 1), 0)
        own_row = lax.shift_right_logical(token, 6)
        own_col = lax.bitwise_and(lax.shift_right_logical(token, 2), 3)
        place = lax.broadcasted_iota(jnp.int32, (1, count), 1) + first
        second = place >= AREA
        j = jnp.where(second, place - AREA, place)
        r_row = 2 - 3 * r
        side = jnp.where(j >= E_AT, j - E_AT, j - L_AT)
        side_row = jnp.where(side >= EDGE, r_row, lax.shift_right_arithmetic(side, 4))
        area_row = jnp.where(
            j >= L_AT, side_row, jnp.where(j >= R_AT, r_row, lax.shift_right_logical(j, 6))
        )
        area_col = jnp.where(
            j >= E_AT, 4,
            jnp.where(j >= L_AT, -1, lax.bitwise_and(lax.shift_right_logical(j, 2), 3)),
        )
        whole_col = area_col + 4 * c
        inside = (whole_col >= 0) & (whole_col < 4 * n_cols)
        dr = area_row - own_row
        dc = area_col - own_col
        close = (dr >= -1) & (dr <= 1) & (dc >= -1) & (dc <= 1) & inside
        return jnp.where(close, 3 * dr + dc + 4, -1), second

    def bias(first, count, source, ok, turned):
        code, second = codes(first, count)
        allow = jnp.zeros((OWN, count), jnp.int32)
        for o in range(9):
            own_ok = 1 if o == 4 else window[o, 1, p]
            entry = jnp.where(second, window[o, 0, source] * ok, own_ok)
            allow = jnp.where(code == (8 - o if turned else o), entry, allow)
        return jnp.where(allow > 0, 0.0, NEG)

    def masks():
        later = jnp.minimum(p + 1, periods - 1)
        back_ok = link[p] * (p > 0).astype(jnp.int32)
        ahead_ok = link[later] * (p + 1 < periods).astype(jnp.int32)
        bias_f[...] = bias(0, 2 * AREA, p, back_ok, False)
        bias_b[...] = bias(0, MAIN, later, ahead_ok, True)
        bias_rest[...] = bias(MAIN, REST, later, ahead_ok, True)

    lane = lax.broadcasted_iota(jnp.int32, (OWN, 128), 1)
    lane16 = lax.bitwise_and(lane, 15)

    def forward(h, total_stats):
        ch = pl.ds(pl.multiple_of(h * HD, HD), HD)
        vh = pl.ds(pl.multiple_of(channels + h * HD, HD), HD)
        scores = nt(qg[:OWN, ch], kv[:, ch]) * scale + bias_f[...]
        peak = jnp.max(scores, axis=1, keepdims=True)
        e = jnp.exp(scores - peak)
        total = jnp.sum(e, axis=1, keepdims=True)
        weights = e * (1.0 / total)
        out = nn(weights.astype(BF16), kv[:, vh]).astype(BF16)
        o_ref[:, ch] = out
        g = qg[:OWN, vh]
        delta = jnp.sum(g.astype(F32) * out.astype(F32), axis=1, keepdims=True)
        ds = (weights * (nt(g, kv[:, vh]) - delta)).astype(BF16)
        dq_ref[:, ch] = (nn(ds, kv[:, ch]) * scale).astype(BF16)
        total_stats = jnp.where(lane16 == h, peak + jnp.log(total), total_stats)
        return jnp.where(lane16 == h + heads, delta, total_stats)

    saves = []

    def save(pairs):
        for src, dst in pairs:
            op = pltpu.make_async_copy(src, dst, local.at[4 + len(saves)])
            op.start()
            saves.append(op)

    result = []

    def run_forward():
        zero = jnp.zeros((OWN, 128), F32)
        result.append(lax.fori_loop(0, heads, forward, zero, unroll=UNROLL))

    sops, slefts, srights = [], [], []

    def send_stats():
        value = result[0]
        hi = value.astype(BF16).astype(F32)
        mid = (value - hi).astype(BF16).astype(F32)
        low = value - hi - mid
        parts = jnp.where(lane < 16, hi, jnp.where(lane < 32, mid, low)).astype(BF16)
        sown[...] = parts
        stats[:OWN, :] = parts
        spack[...] = nn(edge_pick(ROWS), parts).astype(BF16)

        def stat(kept, src, at, size, device):
            i = len(sops) + len(slefts) + len(srights)
            op = copy(src, stats.at[pl.ds(at, size)], ssend, srecv, i, device)
            kept.append(op)

        right_corner = pl.multiple_of(EDGE + corner_at, CORNER)
        for base, t in ((0, p), (AREA, prv)):
            stat(sops, sown.at[pl.ds(half_at, HALF)], base + R_AT, HALF, (t, mate, c))
            stat(slefts, spack.at[pl.ds(corner_at, CORNER)], base + E_AT + EDGE, CORNER, (t, mate, left))
            stat(srights, spack.at[pl.ds(right_corner, CORNER)], base + L_AT + EDGE, CORNER, (t, mate, right))
            stat(slefts, spack.at[pl.ds(0, EDGE)], base + E_AT, EDGE, (t, r, left))
            stat(srights, spack.at[pl.ds(EDGE, EDGE)], base + L_AT, EDGE, (t, r, right))
        stat(sops, sown, AREA, OWN, (prv, r, c))
        for op in sops:
            op.start()

        @pl.when(has_left)
        def _():
            for op in slefts:
                op.start()

        @pl.when(has_right)
        def _():
            for op in srights:
                op.start()

        save(((o_ref, o_out), (dq_ref, dq_out)))

    def rows():
        for op in sops:
            op.wait_recv()

        @pl.when(has_right)
        def _():
            for op in slefts:
                op.wait_recv()

        @pl.when(has_left)
        def _():
            for op in srights:
                op.wait_recv()

        pick_row = lax.broadcasted_iota(jnp.int32, (16, 128), 0)
        pick_lane = lax.broadcasted_iota(jnp.int32, (16, 128), 1)
        same = lax.bitwise_and(pick_lane, 15) == pick_row
        pick = jnp.where(same & (pick_lane < 48), 1.0, 0.0)
        stat_rows[...] = nt(pick.astype(BF16), stats[:MAIN, :])
        return nt(pick.astype(BF16), stats[MAIN:, :])

    def backward(h, at, count, bias_now, lse, delta):
        ch = pl.ds(pl.multiple_of(h * HD, HD), HD)
        vh = pl.ds(pl.multiple_of(channels + h * HD, HD), HD)
        span = pl.ds(at, count)
        scores = nt(kv[:OWN, ch], qg[span, ch]) * scale + bias_now
        weights = jnp.exp(scores - lse)
        dv = nn(weights.astype(BF16), qg[span, vh])
        dp = nt(kv[:OWN, vh], qg[span, vh])
        ds = (weights * (dp - delta)).astype(BF16)
        return nn(ds, qg[span, ch]), dv

    kept = []

    def main_backward():
        kept.append(rows())

        def one(h, carry):
            ch = pl.ds(pl.multiple_of(h * HD, HD), HD)
            lse = stat_rows[pl.ds(h, 1), :]
            delta = stat_rows[pl.ds(h + heads, 1), :]
            dk, dv = backward(h, 0, MAIN, bias_b[...], lse, delta)
            dk_sum[:, ch] = dk
            dv_sum[:, ch] = dv
            return carry

        lax.fori_loop(0, heads, one, 0, unroll=UNROLL)

    def rest_backward():
        for h in range(heads):
            ch = pl.ds(h * HD, HD)
            lse = kept[0][h:h + 1, :]
            delta = kept[0][h + heads:h + heads + 1, :]
            dk, dv = backward(h, MAIN, REST, bias_rest[...], lse, delta)
            dk_ref[:, ch] = ((dk_sum[:, ch] + dk) * scale).astype(BF16)
            dv_ref[:, ch] = (dv_sum[:, ch] + dv).astype(BF16)
        save(((dk_ref, dk_out), (dv_ref, dv_out)))

    def load(x):
        loads[2 * x].wait()
        loads[2 * x + 1].wait()

    steps = {
        "R": begin_r, "T": begin_t, "E": begin_e, "r": after_r, "t": after_t, "tr": after_tr,
        "near": near, "far": far, "load": load, "sent": lambda x: got["R", x].wait_send(),
    }
    plain = {
        "mask": masks, "F": run_forward, "stat": send_stats, "B1": main_backward, "B2": rest_backward,
    }
    done_sends = []
    for word in PLAN:
        if word in plain:
            plain[word]()
        else:
            steps[word[:-1]](int(word[-1]))
            if word[:-1] == "sent":
                done_sends.append(got["R", int(word[-1])])
    for op in pending + sops:
        if not any(op is one for one in done_sends):
            op.wait_send()

    @pl.when(has_left)
    def _():
        for op in lefts + slefts:
            op.wait_send()

    @pl.when(has_right)
    def _():
        for op in rights + srights:
            op.wait_send()

    for op in saves:
        op.wait()


def flush(*refs):
    count = (len(refs) - 2) // 3
    sources, targets, held = refs[:count], refs[count:2 * count], refs[2 * count:3 * count]
    loads = [pltpu.make_async_copy(sources[i], held[i], refs[-2].at[i]) for i in range(count)]
    stores = [pltpu.make_async_copy(held[i], targets[i], refs[-1].at[i]) for i in range(count)]
    for op in loads:
        op.start()
    for load, store in zip(loads, stores):
        load.wait()
        store.start()
    for op in stores:
        op.wait()


def body(query, key, value, out_grad, tile_window, period_link):
    channels = query.shape[-1]
    heads = channels // HD
    flat = [x.reshape(OWN, channels) for x in (query, key, value, out_grad)]
    whole = pl.BlockSpec(memory_space=pltpu.HBM)
    shapes = [jax.ShapeDtypeStruct((OWN, channels), BF16)] * 4
    table = pl.BlockSpec(memory_space=pltpu.SMEM)
    outs = pl.pallas_call(
        functools.partial(
            kernel, heads=heads, periods=lax.axis_size("tm"), n_cols=lax.axis_size("col")
        ),
        out_shape=shapes,
        in_specs=[table, table] + [whole] * 4,
        out_specs=[whole] * 4,
        scratch_shapes=[
            pltpu.VMEM((2 * AREA, 2 * channels), BF16),
            pltpu.VMEM((2 * AREA, 2 * channels), BF16),
            pltpu.VMEM((2 * AREA, 128), BF16),
            pltpu.VMEM((2, 2 * EDGE, 2 * channels), BF16),
            pltpu.VMEM((2, 2 * CORNER, 2 * channels), BF16),
            pltpu.VMEM((2, 2 * EDGE, 2 * channels), BF16),
            pltpu.VMEM((2, 2 * CORNER, 2 * channels), BF16),
            pltpu.VMEM((2 * EDGE, 128), BF16),
            pltpu.VMEM((OWN, 128), BF16),
            pltpu.VMEM((OWN, 2 * AREA), F32),
            pltpu.VMEM((OWN, MAIN), F32),
            pltpu.VMEM((OWN, REST), F32),
            pltpu.VMEM((2 * heads, MAIN), F32),
            pltpu.VMEM((OWN, channels), BF16),
            pltpu.VMEM((OWN, channels), BF16),
            pltpu.VMEM((OWN, channels), BF16),
            pltpu.VMEM((OWN, channels), BF16),
            pltpu.VMEM((OWN, channels), F32),
            pltpu.VMEM((OWN, channels), F32),
            pltpu.SemaphoreType.DMA((8,)),
            pltpu.SemaphoreType.DMA((22,)),
            pltpu.SemaphoreType.DMA((22,)),
            pltpu.SemaphoreType.DMA((11,)),
            pltpu.SemaphoreType.DMA((11,)),
        ],
        compiler_params=pltpu.CompilerParams(
            collective_id=0, has_side_effects=True, vmem_limit_bytes=63 * 1024 * 1024
        ),
    )(tile_window.transpose(2, 1, 0), period_link, *flat)
    outs = pl.pallas_call(
        flush,
        out_shape=shapes,
        in_specs=[whole] * 4,
        out_specs=[whole] * 4,
        scratch_shapes=[pltpu.VMEM((OWN, channels), BF16)] * 4 + [pltpu.SemaphoreType.DMA((4,))] * 2,
        compiler_params=pltpu.CompilerParams(vmem_limit_bytes=63 * 1024 * 1024),
    )(*outs)
    return tuple(x.reshape(query.shape) for x in outs)


def solution(mesh):
    spread = P("tm", "row", "col", None)
    return jax.shard_map(
        body,
        mesh=mesh,
        in_specs=(spread, spread, spread, spread, P(), P()),
        out_specs=(spread, spread, spread, spread),
        check_vma=False,
    )
```

```python
import functools
import math

import jax
import jax.numpy as jnp
from jax import lax
from jax.experimental import pallas as pl
from jax.experimental.pallas import tpu as pltpu
from jax.sharding import PartitionSpec as P

HD = 128
S = 4
ROWS = 8
COLS = 16
OWN = ROWS * COLS
HALF = S * COLS
EDGE = ROWS * S
CORNER = S * S
SIDE = EDGE + CORNER
AREA = OWN + HALF + 2 * SIDE
R_AT = OWN
L_AT = OWN + HALF
E_AT = L_AT + SIDE
NEG = -1e30
MESH = pl.DeviceIdType.MESH
F32 = jnp.float32
BF16 = jnp.bfloat16

UNROLL = 8
MAIN = AREA + OWN
REST = 2 * AREA - MAIN
PLAN = (
    "load0", "R0", "T0", "E0", "load1", "mask", "E1", "r0", "t0", "R1", "near0", "F1", "tr0",
    "T1", "far0", "F", "stat", "r1", "t1", "near1", "B1", "tr1", "far1", "B2",
)


def nt(a, b):
    return lax.dot_general(a, b, (((1,), (1,)), ((), ())), preferred_element_type=F32)


def nn(a, b):
    return lax.dot_general(a, b, (((1,), (0,)), ((), ())), preferred_element_type=F32)


def edge_pick(rows):
    count = rows * S
    out = lax.broadcasted_iota(jnp.int32, (2 * count, rows * COLS), 0)
    src = lax.broadcasted_iota(jnp.int32, (2 * count, rows * COLS), 1)
    right = (out >= count).astype(jnp.int32)
    place = out - right * count
    want = lax.shift_right_logical(place, 2) * COLS + lax.bitwise_and(place, 3) + right * (COLS - S)
    return jnp.where(src == want, 1.0, 0.0).astype(BF16)


def kernel(
    window, link, q_ref, k_ref, v_ref, g_ref, o_out, dq_out, dk_out, dv_out,
    kv, qg, stats, pack_own, pack_r, pack_t, pack_tr, spack, sown, bias_f, bias_f2, bias_b, bias_rest,
    stat_rows, o_ref, dq_ref, dk_ref, dv_ref, dk_sum, dv_sum, early_s, early_g,
    local, send, recv, ssend, srecv, *, heads, periods, n_cols,
):
    channels = heads * HD
    scale = 1.0 / math.sqrt(HD)
    p = lax.axis_index("tm")
    r = lax.axis_index("row")
    c = lax.axis_index("col")
    nxt = lax.rem(p + 1, periods)
    prv = lax.rem(p + periods - 1, periods)
    mate = 1 - r
    has_left = c > 0
    has_right = c < n_cols - 1
    left = jnp.maximum(c - 1, 0)
    right = jnp.minimum(c + 1, n_cols - 1)
    bufs = (kv, qg)
    toward = (nxt, prv)

    loads = []
    for i, (src, buf, at) in enumerate(
        ((k_ref, kv, 0), (v_ref, kv, channels), (q_ref, qg, 0), (g_ref, qg, channels))
    ):
        op = pltpu.make_async_copy(src, buf.at[pl.ds(0, OWN), pl.ds(at, channels)], local.at[i])
        op.start()
        loads.append(op)

    barrier = pltpu.get_barrier_semaphore()

    def greet(*friends):
        for friend in friends:
            pl.semaphore_signal(barrier, inc=1, device_id=friend, device_id_type=MESH)

    greet((p, mate, c), (nxt, r, c), (prv, r, c), (nxt, mate, c), (prv, mate, c))

    @pl.when(has_left)
    def _():
        greet(*[(t, row, left) for t in (p, nxt, prv) for row in (r, mate)])

    @pl.when(has_right)
    def _():
        greet(*[(t, row, right) for t in (p, nxt, prv) for row in (r, mate)])

    both = 5 + 6 * has_left.astype(jnp.int32) + 6 * has_right.astype(jnp.int32)
    pl.semaphore_wait(barrier, both)

    for missing, at in ((has_left, L_AT), (has_right, E_AT)):

        @pl.when(jnp.logical_not(missing))
        def _():
            for base in (0, AREA):
                for buf in (kv, qg):
                    buf[pl.ds(base + at, SIDE), :] = jnp.zeros((SIDE, 2 * channels), BF16)
                stats[pl.ds(base + at, SIDE), :] = jnp.zeros((SIDE, 128), BF16)

    half_at = pl.multiple_of(HALF * (1 - r), HALF)
    corner_at = pl.multiple_of(CORNER * (1 - r), CORNER)
    NAMES = ("R", "T", "TR", "le", "re", "lc", "rc", "tle", "tre", "tlc", "trc")
    pending, lefts, rights = [], [], []

    def copy(src, dst, a, b, i, device):
        return pltpu.make_async_remote_copy(
            src_ref=src, dst_ref=dst, send_sem=a.at[i], recv_sem=b.at[i],
            device_id=device, device_id_type=MESH,
        )

    got = {}

    def make(x, name, src, at, size, device):
        op = copy(src, bufs[x].at[pl.ds(at, size)], send, recv, x * 11 + NAMES.index(name), device)
        got[name, x] = op
        return op

    def go(*args):
        op = make(*args)
        op.start()
        pending.append(op)

    def sides(x, tag, pack, rows, base, shift):
        count = rows * S
        a = make(x, tag[0], pack.at[x, pl.ds(0, count)], base + E_AT + shift, count, (p, r, left))
        b = make(x, tag[1], pack.at[x, pl.ds(count, count)], base + L_AT + shift, count, (p, r, right))
        pl.when(has_left)(a.start)
        pl.when(has_right)(b.start)
        lefts.append(a)
        rights.append(b)

    def begin_r(x):
        go(x, "R", bufs[x].at[pl.ds(half_at, HALF)], R_AT, HALF, (p, mate, c))

    def begin_t(x):
        go(x, "T", bufs[x].at[pl.ds(0, OWN)], AREA, OWN, (toward[x], r, c))

    def begin_e(x):
        pack_own[x] = nn(edge_pick(ROWS), bufs[x][:OWN, :]).astype(BF16)
        sides(x, ("le", "re"), pack_own, ROWS, 0, 0)

    def after_r(x):
        got["R", x].wait_recv()
        turn = lax.rem(p, 8) == (7 if x == 0 else 0)
        at = pl.multiple_of(jnp.where(turn, half_at, R_AT), HALF)
        row = jnp.where(turn, mate, r)
        go(x, "TR", bufs[x].at[pl.ds(at, HALF)], AREA + R_AT, HALF, (toward[x], row, c))
        pack_r[x] = nn(edge_pick(S), bufs[x][R_AT:L_AT, :]).astype(BF16)
        sides(x, ("lc", "rc"), pack_r, S, 0, EDGE)

    def after_t(x):
        got["T", x].wait_recv()
        pack_t[x] = nn(edge_pick(ROWS), bufs[x][AREA:AREA + OWN, :]).astype(BF16)
        sides(x, ("tle", "tre"), pack_t, ROWS, AREA, 0)

    def after_tr(x):
        got["TR", x].wait_recv()
        pack_tr[x] = nn(edge_pick(S), bufs[x][AREA + R_AT:AREA + L_AT, :]).astype(BF16)
        sides(x, ("tlc", "trc"), pack_tr, S, AREA, EDGE)

    def arrived(x, from_right, from_left):
        @pl.when(has_right)
        def _():
            for name in from_right:
                got[name, x].wait_recv()

        @pl.when(has_left)
        def _():
            for name in from_left:
                got[name, x].wait_recv()

    def near(x):
        arrived(x, ("le", "lc"), ("re", "rc"))

    def far(x):
        arrived(x, ("tle", "tlc"), ("tre", "trc"))

    def codes(first, count):
        token = lax.broadcasted_iota(jnp.int32, (OWN, 1), 0)
        own_row = lax.shift_right_logical(token, 6)
        own_col = lax.bitwise_and(lax.shift_right_logical(token, 2), 3)
        place = lax.broadcasted_iota(jnp.int32, (1, count), 1) + first
        second = place >= AREA
        j = jnp.where(second, place - AREA, place)
        r_row = 2 - 3 * r
        side = jnp.where(j >= E_AT, j - E_AT, j - L_AT)
        side_row = jnp.where(side >= EDGE, r_row, lax.shift_right_arithmetic(side, 4))
        area_row = jnp.where(
            j >= L_AT, side_row, jnp.where(j >= R_AT, r_row, lax.shift_right_logical(j, 6))
        )
        area_col = jnp.where(
            j >= E_AT, 4,
            jnp.where(j >= L_AT, -1, lax.bitwise_and(lax.shift_right_logical(j, 2), 3)),
        )
        whole_col = area_col + 4 * c
        inside = (whole_col >= 0) & (whole_col < 4 * n_cols)
        dr = area_row - own_row
        dc = area_col - own_col
        close = (dr >= -1) & (dr <= 1) & (dc >= -1) & (dc <= 1) & inside
        return jnp.where(close, 3 * dr + dc + 4, -1), second

    def bias(first, count, source, ok, turned):
        code, second = codes(first, count)
        allow = jnp.zeros((OWN, count), jnp.int32)
        for o in range(9):
            own_ok = 1 if o == 4 else window[o, 1, p]
            entry = jnp.where(second, window[o, 0, source] * ok, own_ok)
            allow = jnp.where(code == (8 - o if turned else o), entry, allow)
        return jnp.where(allow > 0, 0.0, NEG)

    def masks():
        later = jnp.minimum(p + 1, periods - 1)
        back_ok = link[p] * (p > 0).astype(jnp.int32)
        ahead_ok = link[later] * (p + 1 < periods).astype(jnp.int32)
        bias_f[...] = bias(0, MAIN, p, back_ok, False)
        bias_f2[...] = bias(MAIN, REST, p, back_ok, False)
        bias_b[...] = bias(0, MAIN, later, ahead_ok, True)
        bias_rest[...] = bias(MAIN, REST, later, ahead_ok, True)

    lane = lax.broadcasted_iota(jnp.int32, (OWN, 128), 1)
    lane16 = lax.bitwise_and(lane, 15)

    def early_forward():
        def one(h, carry):
            ch = pl.ds(pl.multiple_of(h * HD, HD), HD)
            vh = pl.ds(pl.multiple_of(channels + h * HD, HD), HD)
            early_s[h] = nt(qg[:OWN, ch], kv[:MAIN, ch]) * scale + bias_f[...]
            early_g[h] = nt(qg[:OWN, vh], kv[:MAIN, vh])
            return carry

        lax.fori_loop(0, heads, one, 0, unroll=UNROLL)

    def forward(h, total_stats):
        ch = pl.ds(pl.multiple_of(h * HD, HD), HD)
        vh = pl.ds(pl.multiple_of(channels + h * HD, HD), HD)
        s1 = early_s[h]
        s2 = nt(qg[:OWN, ch], kv[MAIN:, ch]) * scale + bias_f2[...]
        peak = jnp.maximum(jnp.max(s1, axis=1, keepdims=True), jnp.max(s2, axis=1, keepdims=True))
        e1 = jnp.exp(s1 - peak)
        e2 = jnp.exp(s2 - peak)
        total = jnp.sum(e1, axis=1, keepdims=True) + jnp.sum(e2, axis=1, keepdims=True)
        inverse = 1.0 / total
        w1 = e1 * inverse
        w2 = e2 * inverse
        out = nn(w1.astype(BF16), kv[:MAIN, vh]) + nn(w2.astype(BF16), kv[MAIN:, vh])
        out = out.astype(BF16)
        o_ref[:, ch] = out
        g = qg[:OWN, vh]
        delta = jnp.sum(g.astype(F32) * out.astype(F32), axis=1, keepdims=True)
        d1 = (w1 * (early_g[h] - delta)).astype(BF16)
        d2 = (w2 * (nt(g, kv[MAIN:, vh]) - delta)).astype(BF16)
        dq = nn(d1, kv[:MAIN, ch]) + nn(d2, kv[MAIN:, ch])
        dq_ref[:, ch] = (dq * scale).astype(BF16)
        total_stats = jnp.where(lane16 == h, peak + jnp.log(total), total_stats)
        return jnp.where(lane16 == h + heads, delta, total_stats)

    saves = []

    def save(pairs):
        for src, dst in pairs:
            op = pltpu.make_async_copy(src, dst, local.at[4 + len(saves)])
            op.start()
            saves.append(op)

    result = []

    def run_forward():
        zero = jnp.zeros((OWN, 128), F32)
        result.append(lax.fori_loop(0, heads, forward, zero, unroll=UNROLL))

    sops, slefts, srights = [], [], []

    def send_stats():
        value = result[0]
        hi = value.astype(BF16).astype(F32)
        mid = (value - hi).astype(BF16).astype(F32)
        low = value - hi - mid
        parts = jnp.where(lane < 16, hi, jnp.where(lane < 32, mid, low)).astype(BF16)
        sown[...] = parts
        stats[:OWN, :] = parts
        spack[...] = nn(edge_pick(ROWS), parts).astype(BF16)

        def stat(kept, src, at, size, device):
            i = len(sops) + len(slefts) + len(srights)
            op = copy(src, stats.at[pl.ds(at, size)], ssend, srecv, i, device)
            kept.append(op)

        right_corner = pl.multiple_of(EDGE + corner_at, CORNER)
        for base, t in ((0, p), (AREA, prv)):
            stat(sops, sown.at[pl.ds(half_at, HALF)], base + R_AT, HALF, (t, mate, c))
            stat(slefts, spack.at[pl.ds(corner_at, CORNER)], base + E_AT + EDGE, CORNER, (t, mate, left))
            stat(srights, spack.at[pl.ds(right_corner, CORNER)], base + L_AT + EDGE, CORNER, (t, mate, right))
            stat(slefts, spack.at[pl.ds(0, EDGE)], base + E_AT, EDGE, (t, r, left))
            stat(srights, spack.at[pl.ds(EDGE, EDGE)], base + L_AT, EDGE, (t, r, right))
        stat(sops, sown, AREA, OWN, (prv, r, c))
        for op in sops:
            op.start()

        @pl.when(has_left)
        def _():
            for op in slefts:
                op.start()

        @pl.when(has_right)
        def _():
            for op in srights:
                op.start()

        save(((o_ref, o_out), (dq_ref, dq_out)))

    def rows():
        for op in sops:
            op.wait_recv()

        @pl.when(has_right)
        def _():
            for op in slefts:
                op.wait_recv()

        @pl.when(has_left)
        def _():
            for op in srights:
                op.wait_recv()

        pick_row = lax.broadcasted_iota(jnp.int32, (16, 128), 0)
        pick_lane = lax.broadcasted_iota(jnp.int32, (16, 128), 1)
        same = lax.bitwise_and(pick_lane, 15) == pick_row
        pick = jnp.where(same & (pick_lane < 48), 1.0, 0.0)
        stat_rows[...] = nt(pick.astype(BF16), stats[:MAIN, :])
        return nt(pick.astype(BF16), stats[MAIN:, :])

    def backward(h, at, count, bias_now, lse, delta):
        ch = pl.ds(pl.multiple_of(h * HD, HD), HD)
        vh = pl.ds(pl.multiple_of(channels + h * HD, HD), HD)
        span = pl.ds(at, count)
        scores = nt(kv[:OWN, ch], qg[span, ch]) * scale + bias_now
        weights = jnp.exp(scores - lse)
        dv = nn(weights.astype(BF16), qg[span, vh])
        dp = nt(kv[:OWN, vh], qg[span, vh])
        ds = (weights * (dp - delta)).astype(BF16)
        return nn(ds, qg[span, ch]), dv

    kept = []

    def main_backward():
        kept.append(rows())

        def one(h, carry):
            ch = pl.ds(pl.multiple_of(h * HD, HD), HD)
            lse = stat_rows[pl.ds(h, 1), :]
            delta = stat_rows[pl.ds(h + heads, 1), :]
            dk, dv = backward(h, 0, MAIN, bias_b[...], lse, delta)
            dk_sum[:, ch] = dk
            dv_sum[:, ch] = dv
            return carry

        lax.fori_loop(0, heads, one, 0, unroll=UNROLL)

    def rest_backward():
        for h in range(heads):
            ch = pl.ds(h * HD, HD)
            lse = kept[0][h:h + 1, :]
            delta = kept[0][h + heads:h + heads + 1, :]
            dk, dv = backward(h, MAIN, REST, bias_rest[...], lse, delta)
            dk_ref[:, ch] = ((dk_sum[:, ch] + dk) * scale).astype(BF16)
            dv_ref[:, ch] = (dv_sum[:, ch] + dv).astype(BF16)
        save(((dk_ref, dk_out), (dv_ref, dv_out)))

    def load(x):
        loads[2 * x].wait()
        loads[2 * x + 1].wait()

    steps = {
        "R": begin_r, "T": begin_t, "E": begin_e, "r": after_r, "t": after_t, "tr": after_tr,
        "near": near, "far": far, "load": load, "sent": lambda x: got["R", x].wait_send(),
    }
    plain = {
        "mask": masks, "F1": early_forward, "F": run_forward, "stat": send_stats, "B1": main_backward, "B2": rest_backward,
    }
    done_sends = []
    for word in PLAN:
        if word in plain:
            plain[word]()
        else:
            steps[word[:-1]](int(word[-1]))
            if word[:-1] == "sent":
                done_sends.append(got["R", int(word[-1])])
    for op in pending + sops:
        if not any(op is one for one in done_sends):
            op.wait_send()

    @pl.when(has_left)
    def _():
        for op in lefts + slefts:
            op.wait_send()

    @pl.when(has_right)
    def _():
        for op in rights + srights:
            op.wait_send()

    for op in saves:
        op.wait()


def flush(*refs):
    count = (len(refs) - 2) // 3
    sources, targets, held = refs[:count], refs[count:2 * count], refs[2 * count:3 * count]
    loads = [pltpu.make_async_copy(sources[i], held[i], refs[-2].at[i]) for i in range(count)]
    stores = [pltpu.make_async_copy(held[i], targets[i], refs[-1].at[i]) for i in range(count)]
    for op in loads:
        op.start()
    for load, store in zip(loads, stores):
        load.wait()
        store.start()
    for op in stores:
        op.wait()


def body(query, key, value, out_grad, tile_window, period_link):
    channels = query.shape[-1]
    heads = channels // HD
    flat = [x.reshape(OWN, channels) for x in (query, key, value, out_grad)]
    whole = pl.BlockSpec(memory_space=pltpu.HBM)
    shapes = [jax.ShapeDtypeStruct((OWN, channels), BF16)] * 4
    table = pl.BlockSpec(memory_space=pltpu.SMEM)
    outs = pl.pallas_call(
        functools.partial(
            kernel, heads=heads, periods=lax.axis_size("tm"), n_cols=lax.axis_size("col")
        ),
        out_shape=shapes,
        in_specs=[table, table] + [whole] * 4,
        out_specs=[whole] * 4,
        scratch_shapes=[
            pltpu.VMEM((2 * AREA, 2 * channels), BF16),
            pltpu.VMEM((2 * AREA, 2 * channels), BF16),
            pltpu.VMEM((2 * AREA, 128), BF16),
            pltpu.VMEM((2, 2 * EDGE, 2 * channels), BF16),
            pltpu.VMEM((2, 2 * CORNER, 2 * channels), BF16),
            pltpu.VMEM((2, 2 * EDGE, 2 * channels), BF16),
            pltpu.VMEM((2, 2 * CORNER, 2 * channels), BF16),
            pltpu.VMEM((2 * EDGE, 128), BF16),
            pltpu.VMEM((OWN, 128), BF16),
            pltpu.VMEM((OWN, MAIN), F32),
            pltpu.VMEM((OWN, REST), F32),
            pltpu.VMEM((OWN, MAIN), F32),
            pltpu.VMEM((OWN, REST), F32),
            pltpu.VMEM((2 * heads, MAIN), F32),
            pltpu.VMEM((OWN, channels), BF16),
            pltpu.VMEM((OWN, channels), BF16),
            pltpu.VMEM((OWN, channels), BF16),
            pltpu.VMEM((OWN, channels), BF16),
            pltpu.VMEM((OWN, channels), F32),
            pltpu.VMEM((OWN, channels), F32),
            pltpu.VMEM((heads, OWN, MAIN), F32),
            pltpu.VMEM((heads, OWN, MAIN), F32),
            pltpu.SemaphoreType.DMA((8,)),
            pltpu.SemaphoreType.DMA((22,)),
            pltpu.SemaphoreType.DMA((22,)),
            pltpu.SemaphoreType.DMA((11,)),
            pltpu.SemaphoreType.DMA((11,)),
        ],
        compiler_params=pltpu.CompilerParams(
            collective_id=0, has_side_effects=True, vmem_limit_bytes=63 * 1024 * 1024
        ),
    )(tile_window.transpose(2, 1, 0), period_link, *flat)
    outs = pl.pallas_call(
        flush,
        out_shape=shapes,
        in_specs=[whole] * 4,
        out_specs=[whole] * 4,
        scratch_shapes=[pltpu.VMEM((OWN, channels), BF16)] * 4 + [pltpu.SemaphoreType.DMA((4,))] * 2,
        compiler_params=pltpu.CompilerParams(vmem_limit_bytes=63 * 1024 * 1024),
    )(*outs)
    return tuple(x.reshape(query.shape) for x in outs)


def solution(mesh):
    spread = P("tm", "row", "col", None)
    return jax.shard_map(
        body,
        mesh=mesh,
        in_specs=(spread, spread, spread, spread, P(), P()),
        out_specs=(spread, spread, spread, spread),
        check_vma=False,
    )
```

```python
import functools
import math

import jax
import jax.numpy as jnp
from jax import lax
from jax.experimental import pallas as pl
from jax.experimental.pallas import tpu as pltpu
from jax.sharding import PartitionSpec as P

HD = 128
S = 4
ROWS = 8
COLS = 16
OWN = ROWS * COLS
HALF = S * COLS
EDGE = ROWS * S
CORNER = S * S
SIDE = EDGE + CORNER
AREA = OWN + HALF + 2 * SIDE
R_AT = OWN
L_AT = OWN + HALF
E_AT = L_AT + SIDE
NEG = -1e30
MESH = pl.DeviceIdType.MESH
F32 = jnp.float32
BF16 = jnp.bfloat16

UNROLL = 8
MAIN = AREA + OWN
REST = 2 * AREA - MAIN
PLAN = (
    "load0", "R0", "T0", "E0", "load1", "mask", "E1", "r0", "t0", "R1", "tr0", "T1", "near0",
    "far0", "F", "stat", "r1", "t1", "near1", "B1", "tr1", "far1", "B2",
)


def nt(a, b):
    return lax.dot_general(a, b, (((1,), (1,)), ((), ())), preferred_element_type=F32)


def nn(a, b):
    return lax.dot_general(a, b, (((1,), (0,)), ((), ())), preferred_element_type=F32)


def edge_pick(rows):
    count = rows * S
    out = lax.broadcasted_iota(jnp.int32, (2 * count, rows * COLS), 0)
    src = lax.broadcasted_iota(jnp.int32, (2 * count, rows * COLS), 1)
    right = (out >= count).astype(jnp.int32)
    place = out - right * count
    want = lax.shift_right_logical(place, 2) * COLS + lax.bitwise_and(place, 3) + right * (COLS - S)
    return jnp.where(src == want, 1.0, 0.0).astype(BF16)


def kernel(
    window, link, q_ref, k_ref, v_ref, g_ref, o_out, dq_out, dk_out, dv_out,
    kv, qg, stats, pack_own, pack_r, pack_t, pack_tr, spack, sown, bias_f, bias_b, bias_rest,
    stat_rows, o_ref, dq_ref, dk_ref, dv_ref, dk_sum, dv_sum,
    local, send, recv, ssend, srecv, *, heads, periods, n_cols,
):
    channels = heads * HD
    scale = 1.0 / math.sqrt(HD)
    p = lax.axis_index("tm")
    r = lax.axis_index("row")
    c = lax.axis_index("col")
    nxt = lax.rem(p + 1, periods)
    prv = lax.rem(p + periods - 1, periods)
    mate = 1 - r
    has_left = c > 0
    has_right = c < n_cols - 1
    left = jnp.maximum(c - 1, 0)
    right = jnp.minimum(c + 1, n_cols - 1)
    bufs = (kv, qg)
    toward = (nxt, prv)

    loads = []
    for i, (src, buf, at) in enumerate(
        ((k_ref, kv, 0), (v_ref, kv, channels), (q_ref, qg, 0), (g_ref, qg, channels))
    ):
        op = pltpu.make_async_copy(src, buf.at[pl.ds(0, OWN), pl.ds(at, channels)], local.at[i])
        op.start()
        loads.append(op)

    barrier = pltpu.get_barrier_semaphore()

    def greet(*friends):
        for friend in friends:
            pl.semaphore_signal(barrier, inc=1, device_id=friend, device_id_type=MESH)

    greet((p, mate, c), (nxt, r, c), (prv, r, c), (nxt, mate, c), (prv, mate, c))

    @pl.when(has_left)
    def _():
        greet(*[(t, row, left) for t in (p, nxt, prv) for row in (r, mate)])

    @pl.when(has_right)
    def _():
        greet(*[(t, row, right) for t in (p, nxt, prv) for row in (r, mate)])

    both = 5 + 6 * has_left.astype(jnp.int32) + 6 * has_right.astype(jnp.int32)
    pl.semaphore_wait(barrier, both)

    for missing, at in ((has_left, L_AT), (has_right, E_AT)):

        @pl.when(jnp.logical_not(missing))
        def _():
            for base in (0, AREA):
                for buf in (kv, qg):
                    buf[pl.ds(base + at, SIDE), :] = jnp.zeros((SIDE, 2 * channels), BF16)
                stats[pl.ds(base + at, SIDE), :] = jnp.zeros((SIDE, 128), BF16)

    half_at = pl.multiple_of(HALF * (1 - r), HALF)
    corner_at = pl.multiple_of(CORNER * (1 - r), CORNER)
    NAMES = ("R", "T", "TR", "le", "re", "lc", "rc", "tle", "tre", "tlc", "trc")
    pending, lefts, rights = [], [], []

    def copy(src, dst, a, b, i, device):
        return pltpu.make_async_remote_copy(
            src_ref=src, dst_ref=dst, send_sem=a.at[i], recv_sem=b.at[i],
            device_id=device, device_id_type=MESH,
        )

    got = {}

    def make(x, name, src, at, size, device):
        op = copy(src, bufs[x].at[pl.ds(at, size)], send, recv, x * 11 + NAMES.index(name), device)
        got[name, x] = op
        return op

    def go(*args):
        op = make(*args)
        op.start()
        pending.append(op)

    def sides(x, tag, pack, rows, base, shift):
        count = rows * S
        a = make(x, tag[0], pack.at[x, pl.ds(0, count)], base + E_AT + shift, count, (p, r, left))
        b = make(x, tag[1], pack.at[x, pl.ds(count, count)], base + L_AT + shift, count, (p, r, right))
        pl.when(has_left)(a.start)
        pl.when(has_right)(b.start)
        lefts.append(a)
        rights.append(b)

    def begin_r(x):
        go(x, "R", bufs[x].at[pl.ds(half_at, HALF)], R_AT, HALF, (p, mate, c))

    def begin_t(x):
        go(x, "T", bufs[x].at[pl.ds(0, OWN)], AREA, OWN, (toward[x], r, c))

    def begin_e(x):
        pack_own[x] = nn(edge_pick(ROWS), bufs[x][:OWN, :]).astype(BF16)
        sides(x, ("le", "re"), pack_own, ROWS, 0, 0)

    def after_r(x):
        got["R", x].wait_recv()
        turn = lax.rem(p, 8) == (7 if x == 0 else 0)
        at = pl.multiple_of(jnp.where(turn, half_at, R_AT), HALF)
        row = jnp.where(turn, mate, r)
        go(x, "TR", bufs[x].at[pl.ds(at, HALF)], AREA + R_AT, HALF, (toward[x], row, c))
        pack_r[x] = nn(edge_pick(S), bufs[x][R_AT:L_AT, :]).astype(BF16)
        sides(x, ("lc", "rc"), pack_r, S, 0, EDGE)

    def after_t(x):
        got["T", x].wait_recv()
        pack_t[x] = nn(edge_pick(ROWS), bufs[x][AREA:AREA + OWN, :]).astype(BF16)
        sides(x, ("tle", "tre"), pack_t, ROWS, AREA, 0)

    def after_tr(x):
        got["TR", x].wait_recv()
        pack_tr[x] = nn(edge_pick(S), bufs[x][AREA + R_AT:AREA + L_AT, :]).astype(BF16)
        sides(x, ("tlc", "trc"), pack_tr, S, AREA, EDGE)

    def arrived(x, from_right, from_left):
        @pl.when(has_right)
        def _():
            for name in from_right:
                got[name, x].wait_recv()

        @pl.when(has_left)
        def _():
            for name in from_left:
                got[name, x].wait_recv()

    def near(x):
        arrived(x, ("le", "lc"), ("re", "rc"))

    def far(x):
        arrived(x, ("tle", "tlc"), ("tre", "trc"))

    def codes(first, count):
        token = lax.broadcasted_iota(jnp.int32, (OWN, 1), 0)
        own_row = lax.shift_right_logical(token, 6)
        own_col = lax.bitwise_and(lax.shift_right_logical(token, 2), 3)
        place = lax.broadcasted_iota(jnp.int32, (1, count), 1) + first
        second = place >= AREA
        j = jnp.where(second, place - AREA, place)
        r_row = 2 - 3 * r
        side = jnp.where(j >= E_AT, j - E_AT, j - L_AT)
        side_row = jnp.where(side >= EDGE, r_row, lax.shift_right_arithmetic(side, 4))
        area_row = jnp.where(
            j >= L_AT, side_row, jnp.where(j >= R_AT, r_row, lax.shift_right_logical(j, 6))
        )
        area_col = jnp.where(
            j >= E_AT, 4,
            jnp.where(j >= L_AT, -1, lax.bitwise_and(lax.shift_right_logical(j, 2), 3)),
        )
        whole_col = area_col + 4 * c
        inside = (whole_col >= 0) & (whole_col < 4 * n_cols)
        dr = area_row - own_row
        dc = area_col - own_col
        close = (dr >= -1) & (dr <= 1) & (dc >= -1) & (dc <= 1) & inside
        return jnp.where(close, 3 * dr + dc + 4, -1), second

    def bias(first, count, source, ok, turned):
        code, second = codes(first, count)
        allow = jnp.zeros((OWN, count), jnp.int32)
        for o in range(9):
            own_ok = 1 if o == 4 else window[o, 1, p]
            entry = jnp.where(second, window[o, 0, source] * ok, own_ok)
            allow = jnp.where(code == (8 - o if turned else o), entry, allow)
        return jnp.where(allow > 0, 0.0, NEG)

    def masks():
        later = jnp.minimum(p + 1, periods - 1)
        back_ok = link[p] * (p > 0).astype(jnp.int32)
        ahead_ok = link[later] * (p + 1 < periods).astype(jnp.int32)
        bias_f[...] = bias(0, 2 * AREA, p, back_ok, False)
        bias_b[...] = bias(0, MAIN, later, ahead_ok, True)
        bias_rest[...] = bias(MAIN, REST, later, ahead_ok, True)

    lane = lax.broadcasted_iota(jnp.int32, (OWN, 128), 1)
    lane16 = lax.bitwise_and(lane, 15)

    def forward(h, total_stats):
        ch = pl.ds(pl.multiple_of(h * HD, HD), HD)
        vh = pl.ds(pl.multiple_of(channels + h * HD, HD), HD)
        scores = nt(qg[:OWN, ch], kv[:, ch]) * scale + bias_f[...]
        peak = jnp.max(scores, axis=1, keepdims=True)
        e = jnp.exp(scores - peak)
        total = jnp.sum(e, axis=1, keepdims=True)
        weights = e * (1.0 / total)
        out = nn(weights.astype(BF16), kv[:, vh]).astype(BF16)
        o_ref[:, ch] = out
        g = qg[:OWN, vh]
        delta = jnp.sum(g.astype(F32) * out.astype(F32), axis=1, keepdims=True)
        ds = (weights * (nt(g, kv[:, vh]) - delta)).astype(BF16)
        dq_ref[:, ch] = (nn(ds, kv[:, ch]) * scale).astype(BF16)
        total_stats = jnp.where(lane16 == h, peak + jnp.log(total), total_stats)
        return jnp.where(lane16 == h + heads, delta, total_stats)

    saves = []

    def save(pairs):
        for src, dst in pairs:
            op = pltpu.make_async_copy(src, dst, local.at[4 + len(saves)])
            op.start()
            saves.append(op)

    result = []

    def run_forward():
        zero = jnp.zeros((OWN, 128), F32)
        result.append(lax.fori_loop(0, heads, forward, zero, unroll=UNROLL))

    sops, slefts, srights = [], [], []

    def send_stats():
        value = result[0]
        hi = value.astype(BF16).astype(F32)
        mid = (value - hi).astype(BF16).astype(F32)
        low = value - hi - mid
        parts = jnp.where(lane < 16, hi, jnp.where(lane < 32, mid, low)).astype(BF16)
        sown[...] = parts
        stats[:OWN, :] = parts
        spack[...] = nn(edge_pick(ROWS), parts).astype(BF16)

        def stat(kept, src, at, size, device):
            i = len(sops) + len(slefts) + len(srights)
            op = copy(src, stats.at[pl.ds(at, size)], ssend, srecv, i, device)
            kept.append(op)

        right_corner = pl.multiple_of(EDGE + corner_at, CORNER)
        for base, t in ((0, p), (AREA, prv)):
            stat(sops, sown.at[pl.ds(half_at, HALF)], base + R_AT, HALF, (t, mate, c))
            stat(slefts, spack.at[pl.ds(corner_at, CORNER)], base + E_AT + EDGE, CORNER, (t, mate, left))
            stat(srights, spack.at[pl.ds(right_corner, CORNER)], base + L_AT + EDGE, CORNER, (t, mate, right))
            stat(slefts, spack.at[pl.ds(0, EDGE)], base + E_AT, EDGE, (t, r, left))
            stat(srights, spack.at[pl.ds(EDGE, EDGE)], base + L_AT, EDGE, (t, r, right))
        stat(sops, sown, AREA, OWN, (prv, r, c))
        for op in sops:
            op.start()

        @pl.when(has_left)
        def _():
            for op in slefts:
                op.start()

        @pl.when(has_right)
        def _():
            for op in srights:
                op.start()

        save(((o_ref, o_out), (dq_ref, dq_out)))

    def rows():
        for op in sops:
            op.wait_recv()

        @pl.when(has_right)
        def _():
            for op in slefts:
                op.wait_recv()

        @pl.when(has_left)
        def _():
            for op in srights:
                op.wait_recv()

        pick_row = lax.broadcasted_iota(jnp.int32, (16, 128), 0)
        pick_lane = lax.broadcasted_iota(jnp.int32, (16, 128), 1)
        same = lax.bitwise_and(pick_lane, 15) == pick_row
        pick = jnp.where(same & (pick_lane < 48), 1.0, 0.0)
        stat_rows[...] = nt(pick.astype(BF16), stats[:MAIN, :])
        return nt(pick.astype(BF16), stats[MAIN:, :])

    def backward(h, at, count, bias_now, lse, delta):
        ch = pl.ds(pl.multiple_of(h * HD, HD), HD)
        vh = pl.ds(pl.multiple_of(channels + h * HD, HD), HD)
        span = pl.ds(at, count)
        scores = nt(kv[:OWN, ch], qg[span, ch]) * scale + bias_now
        weights = jnp.exp(scores - lse)
        dv = nn(weights.astype(BF16), qg[span, vh])
        dp = nt(kv[:OWN, vh], qg[span, vh])
        ds = (weights * (dp - delta)).astype(BF16)
        return nn(ds, qg[span, ch]), dv

    kept = []

    def main_backward():
        kept.append(rows())

        def one(h, carry):
            ch = pl.ds(pl.multiple_of(h * HD, HD), HD)
            lse = stat_rows[pl.ds(h, 1), :]
            delta = stat_rows[pl.ds(h + heads, 1), :]
            dk, dv = backward(h, 0, MAIN, bias_b[...], lse, delta)
            dk_sum[:, ch] = dk
            dv_sum[:, ch] = dv
            return carry

        lax.fori_loop(0, heads, one, 0, unroll=UNROLL)

    def rest_backward():
        for h in range(heads):
            ch = pl.ds(h * HD, HD)
            lse = kept[0][h:h + 1, :]
            delta = kept[0][h + heads:h + heads + 1, :]
            dk, dv = backward(h, MAIN, REST, bias_rest[...], lse, delta)
            dk_ref[:, ch] = ((dk_sum[:, ch] + dk) * scale).astype(BF16)
            dv_ref[:, ch] = (dv_sum[:, ch] + dv).astype(BF16)
            if h % 4 == 3:
                half = (pl.ds(0, OWN), pl.ds((h - 3) * HD, 4 * HD))
                save(((dk_ref.at[half], dk_out.at[half]), (dv_ref.at[half], dv_out.at[half])))

    def load(x):
        loads[2 * x].wait()
        loads[2 * x + 1].wait()

    steps = {
        "R": begin_r, "T": begin_t, "E": begin_e, "r": after_r, "t": after_t, "tr": after_tr,
        "near": near, "far": far, "load": load, "sent": lambda x: got["R", x].wait_send(),
    }
    plain = {
        "mask": masks, "F": run_forward, "stat": send_stats, "B1": main_backward, "B2": rest_backward,
    }
    done_sends = []
    for word in PLAN:
        if word in plain:
            plain[word]()
        else:
            steps[word[:-1]](int(word[-1]))
            if word[:-1] == "sent":
                done_sends.append(got["R", int(word[-1])])
    for op in pending + sops:
        if not any(op is one for one in done_sends):
            op.wait_send()

    @pl.when(has_left)
    def _():
        for op in lefts + slefts:
            op.wait_send()

    @pl.when(has_right)
    def _():
        for op in rights + srights:
            op.wait_send()

    for op in saves:
        op.wait()


def flush(*refs):
    count = (len(refs) - 2) // 3
    sources, targets, held = refs[:count], refs[count:2 * count], refs[2 * count:3 * count]
    loads = [pltpu.make_async_copy(sources[i], held[i], refs[-2].at[i]) for i in range(count)]
    stores = [pltpu.make_async_copy(held[i], targets[i], refs[-1].at[i]) for i in range(count)]
    for op in loads:
        op.start()
    for load, store in zip(loads, stores):
        load.wait()
        store.start()
    for op in stores:
        op.wait()


def body(query, key, value, out_grad, tile_window, period_link):
    channels = query.shape[-1]
    heads = channels // HD
    flat = [x.reshape(OWN, channels) for x in (query, key, value, out_grad)]
    whole = pl.BlockSpec(memory_space=pltpu.HBM)
    shapes = [jax.ShapeDtypeStruct((OWN, channels), BF16)] * 4
    table = pl.BlockSpec(memory_space=pltpu.SMEM)
    outs = pl.pallas_call(
        functools.partial(
            kernel, heads=heads, periods=lax.axis_size("tm"), n_cols=lax.axis_size("col")
        ),
        out_shape=shapes,
        in_specs=[table, table] + [whole] * 4,
        out_specs=[whole] * 4,
        scratch_shapes=[
            pltpu.VMEM((2 * AREA, 2 * channels), BF16),
            pltpu.VMEM((2 * AREA, 2 * channels), BF16),
            pltpu.VMEM((2 * AREA, 128), BF16),
            pltpu.VMEM((2, 2 * EDGE, 2 * channels), BF16),
            pltpu.VMEM((2, 2 * CORNER, 2 * channels), BF16),
            pltpu.VMEM((2, 2 * EDGE, 2 * channels), BF16),
            pltpu.VMEM((2, 2 * CORNER, 2 * channels), BF16),
            pltpu.VMEM((2 * EDGE, 128), BF16),
            pltpu.VMEM((OWN, 128), BF16),
            pltpu.VMEM((OWN, 2 * AREA), F32),
            pltpu.VMEM((OWN, MAIN), F32),
            pltpu.VMEM((OWN, REST), F32),
            pltpu.VMEM((2 * heads, MAIN), F32),
            pltpu.VMEM((OWN, channels), BF16),
            pltpu.VMEM((OWN, channels), BF16),
            pltpu.VMEM((OWN, channels), BF16),
            pltpu.VMEM((OWN, channels), BF16),
            pltpu.VMEM((OWN, channels), F32),
            pltpu.VMEM((OWN, channels), F32),
            pltpu.SemaphoreType.DMA((10,)),
            pltpu.SemaphoreType.DMA((22,)),
            pltpu.SemaphoreType.DMA((22,)),
            pltpu.SemaphoreType.DMA((11,)),
            pltpu.SemaphoreType.DMA((11,)),
        ],
        compiler_params=pltpu.CompilerParams(
            collective_id=0, has_side_effects=True, vmem_limit_bytes=63 * 1024 * 1024
        ),
    )(tile_window.transpose(2, 1, 0), period_link, *flat)
    outs = pl.pallas_call(
        flush,
        out_shape=shapes,
        in_specs=[whole] * 4,
        out_specs=[whole] * 4,
        scratch_shapes=[pltpu.VMEM((OWN, channels), BF16)] * 4 + [pltpu.SemaphoreType.DMA((4,))] * 2,
        compiler_params=pltpu.CompilerParams(vmem_limit_bytes=63 * 1024 * 1024),
    )(*outs)
    return tuple(x.reshape(query.shape) for x in outs)


def solution(mesh):
    spread = P("tm", "row", "col", None)
    return jax.shard_map(
        body,
        mesh=mesh,
        in_specs=(spread, spread, spread, spread, P(), P()),
        out_specs=(spread, spread, spread, spread),
        check_vma=False,
    )
```
